256 devices in a mesh: dp: 16 (over x, y_lo, core), mp: 16 (over z, y_hi).
Axes of the slice: x: 4, y: 4 (y_hi: 2, y_lo: 2; y = y_hi * 2 + y_lo), z: 8, core: 2. Of those that a mesh axis runs over, the one named last changes fastest.
Arguments:
- grads: bfloat16 [16, 64, 512, 512], P('dp', 'mp'), may hold values from -150 to 150, as said below
- owners: int32 [128, 1], P('mp'), may hold values from 0 to 15; in each aligned block of 8 rows (0 to 7, 8 to 15, ...) at most 2 rows name the same one
- roots_prev: bfloat16 [64, 2, 512, 512], P('mp'), may hold values from -1 to 3, as said below
- moment_first: float32 [64, 512, 512], P('mp', 'dp'), may hold values from -1.8 to 1.8
- moment_second: float32 [64, 512, 512], P('mp', 'dp'), may hold values from 0.01 to 1
Outputs:
- update: float32 [64, 512, 512], P('mp', 'dp')
- moment_first_new: float32 [64, 512, 512], P('mp', 'dp')
- moment_second_new: float32 [64, 512, 512], P('mp', 'dp')
- roots_new: bfloat16 [16, 16, 2, 512, 512], P('dp', 'mp')
The draws below stay inside these ranges and needn't reach their ends.
Inputs may be any that keep to these rules, and one draw needn't show every extreme that they name: `owners`: in the 8 statistics of one index of mp no index of dp is named more than 2 times, and one is named exactly 2 times. `grads`: independent entries. `roots_prev`: each matrix is symmetric.
All inputs are finite; a program needn't handle non-finite values.
Results may differ from the reference program's by a relative error of at most 0.001.
The reference program's roundings to bfloat16 on the way (of `grad_half` and `sectioned`) count: a program that leaves them out, or rounds other values in their place, can miss the bound.
Values may be sent and summed in bfloat16 or wider, within the bound.
A program may use at most 128 MiB of HBM per device.

```python
import math
import jax
import jax.numpy as jnp
import numpy as np
from jax import lax

BS = 512
BLK_DEV = 4
CAP = 2
ITERS = 3
NB = 64
MATS = 128
N_DP = 16
N_MP = 16


def draw_grads(key, part):
    key = jax.random.fold_in(key, 11)
    k_noise, k_row, k_col = jax.random.split(key, 3)
    noise_draw = jnp.clip(jax.random.normal(k_noise, (N_DP, NB, BS, BS), jnp.float32), -5.0, 5.0)
    row_rise = jnp.exp(jnp.log(3.0) * jnp.arange(BS, dtype=jnp.float32) / BS)
    row_scale = row_rise[None, :, None] * jnp.exp(jax.random.uniform(k_row, (NB, BS, 1), jnp.float32, 0.0, jnp.log(3.3)))
    col_scale = jnp.exp(jax.random.uniform(k_col, (NB, 1, BS), jnp.float32, 0.0, jnp.log(10.0)))
    block_scale = jnp.exp(jnp.log(3.0) * jnp.arange(NB, dtype=jnp.float32) / max(NB - 1, 1))[:, None, None]
    return (0.1 * noise_draw * row_scale * col_scale * block_scale).astype(jnp.bfloat16)


def draw_roots_prev(key, part):
    key = jax.random.fold_in(key, 23)
    k_diag, k_off = jax.random.split(key, 2)
    diagonal = 0.5 * jnp.exp(jax.random.uniform(k_diag, (NB, 2, BS), jnp.float32, 0.0, jnp.log(4.0)))
    raw_noise = jnp.clip(jax.random.normal(k_off, (NB, 2, BS, BS), jnp.float32), -4.0, 4.0)
    off_diag = 0.4 * 0.7071 / jnp.sqrt(jnp.float32(BS)) * (raw_noise + jnp.swapaxes(raw_noise, -1, -2))
    identity = jnp.eye(BS, dtype=jnp.float32)
    return (off_diag * (1.0 - identity) + diagonal[..., None] * identity).astype(jnp.bfloat16)


def steps_of(own_key, shape, cuts, least, largest):
    def one(axis_at, parts):
        heights = jax.random.uniform(jax.random.fold_in(jax.random.fold_in(own_key, 6), axis_at), (parts,), jnp.float32, least / len(cuts), largest / len(cuts))
        return jnp.repeat(jnp.exp(heights), shape[axis_at] // parts).reshape((-1,) + (1,) * (len(shape) - axis_at - 1))

    loudness = one(*cuts[0])
    for cut in cuts[1:]:
        loudness = loudness * one(*cut)
    return loudness


def deal_out(key, own, number, rows, amount, top, reach, slope):
    sequence = jax.random.permutation(key, amount)
    packed, ordinary = load_shares(amount, rows * top, reach, slope, True), load_shares(amount, rows * top, reach, slope, False)
    places = jnp.arange(amount)

    def named(tallies, offset_by):
        used = int((tallies > 0).sum())
        fixed = max(1, used // 4)
        passed = fixed + (places - fixed + offset_by * (used - fixed)) % max(1, amount - fixed)
        return jnp.zeros((amount,), jnp.int32).at[sequence[jnp.where(places < fixed, places, passed)]].set(jnp.asarray(tallies, jnp.int32))

    tallies = jnp.where(number % 4 == 0, named(packed, number // 4), named(ordinary, number - number // 4 - 1))
    mixed = jax.random.permutation(jax.random.fold_in(own, 3), amount)
    giver, taker = mixed[0:amount // 2 * 2:2], mixed[1:amount // 2 * 2:2]
    margin = jnp.minimum(tallies[giver] - 1, reach - tallies[taker]) // 2
    margin = jnp.where((giver == sequence[0]) | (taker == sequence[0]) | (tallies[taker] == 0), 0, jnp.maximum(margin, 0))
    passed = jax.random.randint(jax.random.fold_in(own, 4), (amount // 2,), 0, 1 << 20) % (margin + 1)
    tallies = tallies.at[giver].add(-passed).at[taker].add(passed)
    items = jnp.searchsorted(jnp.cumsum(tallies), jnp.arange(rows * top), side="right").astype(jnp.int32)
    table = items.reshape(top, rows).T
    table = table[jax.random.permutation(jax.random.fold_in(own, 1), rows)]
    offset_by = jax.random.randint(jax.random.fold_in(own, 2), (rows, 1), 0, top)
    return jnp.take_along_axis(table, (jnp.arange(top)[None, :] + offset_by) % top, axis=1)


def load_shares(amount, total, most, lean, full):
    loads = [(1 << 20) // math.isqrt(rank ** lean) + 1 for rank in range(1, amount + 1)]
    largest = most if full else min(most, max(-(-total // amount), total * loads[0] // sum(loads)))
    least = 1 if total - largest >= amount - 1 else 0
    counts, rest = [largest] + [least] * (amount - 1), total - largest - least * (amount - 1)
    while rest > 0:
        free = [i for i in range(1, amount) if counts[i] < largest] or [i for i in range(1, amount) if counts[i] < most]
        pool, remaining = sum([loads[i] for i in free]), rest
        for i in free:
            addition = min(most - counts[i], max(1, remaining * loads[i] // pool), rest)
            counts[i] = counts[i] + addition
            rest = rest - addition
    return np.array(counts)


def gaussian(key, extent, width, bound, cuts=(), kind=jnp.bfloat16):
    gain = steps_of(key, extent, cuts, -0.22, 0.18) if cuts else 1.0
    array = jax.random.normal(key, extent, jnp.float32) * width * gain
    return jnp.minimum(jnp.maximum(array, -bound), bound).astype(kind)


def setup_inputs(seed: int = 0) -> dict:
    seeds = jax.random.split(jax.random.key(seed), 6)
    grads = draw_grads(jax.random.fold_in(seeds[5], 71), 0)
    owners_keys = jax.random.split(jax.random.fold_in(seeds[1], 1), MATS // (2 * BLK_DEV))
    owners_turns = jax.random.permutation(jax.random.fold_in(seeds[1], 3), MATS // (2 * BLK_DEV))
    owners = jax.vmap(lambda own, number: deal_out(jax.random.fold_in(seeds[1], 2), own, number, 2 * BLK_DEV, N_DP, 1, CAP, 2))(owners_keys, owners_turns).reshape((MATS, 1))
    roots_prev = draw_roots_prev(jax.random.fold_in(seeds[5], 71), 0)
    moment_first = gaussian(seeds[3], (NB, BS, BS), 0.3, 1.8, ((0, 16), (1, 16)), jnp.float32)
    moment_second = jnp.clip(jnp.exp(math.log(1.0) - 4.6051702 * jax.random.uniform(seeds[4], (NB, BS, BS), jnp.float32) ** steps_of(seeds[4], (NB, BS, BS), ((0, 16), (1, 16)), -0.2, 0.2)), 0.01, 1.0)
    return dict(grads=grads, owners=owners, roots_prev=roots_prev, moment_first=moment_first, moment_second=moment_second)


HIGHEST_PRECISION = lax.Precision.HIGHEST

def count_before(labels):
    total_items = labels.shape[0]
    matches = labels[:, None] == labels[None, :]
    row_ids = lax.broadcasted_iota(jnp.int32, (total_items, total_items), 0)
    col_ids = lax.broadcasted_iota(jnp.int32, (total_items, total_items), 1)
    return lax.optimization_barrier(jnp.sum(jnp.where(matches & (col_ids < row_ids), 1, 0), axis=1)).astype(jnp.int32)

def inverse_root(statistic):
    block_order = statistic.shape[-1]
    identity = jnp.eye(block_order, dtype=statistic.dtype)
    shifted = statistic + 0.0001 * identity
    norm_value = jnp.sqrt(jnp.sum(shifted * shifted))
    coupled = shifted / norm_value
    iterate = identity
    for step_id in range(ITERS):
        factor = (5.0 * identity - coupled) / 4.0
        if step_id == 0:
            iterate = factor
        else:
            iterate = jnp.dot(iterate, factor, precision=HIGHEST_PRECISION)
        if step_id + 1 < ITERS:
            factor_sq = jnp.dot(factor, factor, precision=HIGHEST_PRECISION)
            factor_quad = jnp.dot(factor_sq, factor_sq, precision=HIGHEST_PRECISION)
            coupled = jnp.dot(factor_quad, coupled, precision=HIGHEST_PRECISION)
    return iterate

def reference(grads, owners, roots_prev, moment_first, moment_second):

    def per_block(block_id):
        shard_grads = lax.dynamic_index_in_dim(grads, block_id, 1, keepdims=False).astype(jnp.float32)
        left_stat = jnp.einsum('dik,djk->ij', shard_grads, shard_grads, precision=HIGHEST_PRECISION) / N_DP
        right_stat = jnp.einsum('dki,dkj->ij', shard_grads, shard_grads, precision=HIGHEST_PRECISION) / N_DP
        grad_mean = lax.optimization_barrier(jnp.sum(shard_grads, axis=0)) / N_DP
        return (left_stat, right_stat, grad_mean)
    left_all, right_all, grad_mean = lax.map(per_block, jnp.arange(NB, dtype=jnp.int32))
    statistics = jnp.stack((left_all, right_all), axis=1).reshape(MATS, BS, BS)
    roots_all = lax.map(inverse_root, statistics).astype(jnp.bfloat16)
    owner_ids = owners[:, 0].reshape(N_MP, 2 * BLK_DEV)
    slot_ids = jax.vmap(count_before)(owner_ids)
    column_ids = jnp.broadcast_to(jnp.arange(N_MP, dtype=jnp.int32)[:, None], owner_ids.shape)
    roots_new = jnp.zeros((N_DP, N_MP, CAP, BS, BS), jnp.bfloat16)
    roots_new = roots_new.at[owner_ids.reshape(-1), column_ids.reshape(-1), slot_ids.reshape(-1)].set(roots_all)
    grad_half = grad_mean.astype(jnp.bfloat16)
    sectioned = jnp.einsum('bij,bjk->bik', roots_prev[:, 0].astype(jnp.float32), grad_half.astype(jnp.float32), precision=HIGHEST_PRECISION).astype(jnp.bfloat16)
    precond = jnp.einsum('bij,bjk->bik', sectioned.astype(jnp.float32), roots_prev[:, 1].astype(jnp.float32), precision=HIGHEST_PRECISION)
    first_new = 0.9 * moment_first + 0.1 * grad_mean
    second_new = 0.95 * moment_second + 0.05 * grad_mean * grad_mean
    adam_step = first_new / (jnp.sqrt(second_new) + 1e-08)
    graft_ratio = jnp.sqrt(jnp.sum(adam_step * adam_step)) / jnp.sqrt(jnp.sum(precond * precond) + 1e-06)
    return (graft_ratio * precond, first_new, second_new, roots_new)
```

```python
import jax
import jax.numpy as jnp
from jax import lax
from jax.experimental import pallas as pl
from jax.experimental.pallas import tpu as pltpu
from jax.sharding import PartitionSpec as P

MESH = pl.DeviceIdType.MESH
F32 = jnp.float32
BF16 = jnp.bfloat16
BS = 512
T = 128
N_DP = 16
ROWS = BS // N_DP
PIECE = 8 * T
DIAG = 16
OFF_TILES = ((0, 1), (0, 2), (0, 3), (1, 2), (1, 3), (2, 3))
ORDER = (2, 1, 3, 0)

CORE = 0
RAW = 2
STAT = 10
SUMY = 16
DG = 17
GRD = 25
GMX = 28
SCX = 44
AGR = 60
SIB = 64
SC1 = 68
SC2 = 84
AGS = 100
N_SEM = 108
LOC = 8


def dot(a, b):
    return jnp.dot(a, b, preferred_element_type=F32)


def tile_of(t):
    return pl.ds(t * T, T)


def kernel(
    n_mp,
    owners,
    grads,
    roots,
    m1,
    m2,
    update,
    m1n,
    m2n,
    roots_new,
    g_mine,
    g_other,
    left_v,
    right_v,
    tr,
    packed,
    got,
    y_out,
    y_in,
    dg_out,
    dg_in,
    g_send,
    g_recv,
    gm_loc,
    sc_loc,
    gm_rows,
    sc_rows,
    pieces,
    mat,
    mat_b,
    yy,
    yy_b,
    ee,
    ee_b,
    precond,
    s1_out,
    s1_in,
    s2_out,
    s2_in,
    ss,
    rs,
    ls,
):
    me = lax.axis_index("dp")
    col = lax.axis_index("mp")
    x, y, c = me // 4, (me // 2) % 2, me % 2
    even = (x % 2) == c
    keep = x // 2
    blk = 2 * c + y

    def dev(xx, yv, cc):
        return (xx * 4 + yv * 2 + cc, col)

    def xo(k):
        return lax.rem(x + k, 4)

    def rc(src, dst, i_send, i_recv, where):
        return pltpu.make_async_remote_copy(
            src_ref=src,
            dst_ref=dst,
            send_sem=ss.at[i_send],
            recv_sem=rs.at[i_recv],
            device_id=where,
            device_id_type=MESH,
        )

    barrier = pltpu.get_barrier_semaphore()
    for k in range(1, N_DP):
        pl.semaphore_signal(
            barrier, inc=1, device_id=(lax.rem(me + k, N_DP), col), device_id_type=MESH
        )
    for k in range(1, n_mp):
        pl.semaphore_signal(
            barrier, inc=1, device_id=(me, lax.rem(col + k, n_mp)), device_id_type=MESH
        )

    loads = [
        pltpu.make_async_copy(grads.at[0, 2 * c + 1 - y], g_other.at[0], ls.at[0]),
        pltpu.make_async_copy(grads.at[0, 2 * c + y], g_mine.at[0], ls.at[1]),
        pltpu.make_async_copy(roots.at[blk, 0], left_v, ls.at[2]),
    ] + [
        pltpu.make_async_copy(roots.at[b, 1], right_v.at[b], ls.at[3 + b]) for b in range(4)
    ]
    for cp in loads:
        cp.start()
    pl.semaphore_wait(barrier, N_DP - 1 + n_mp - 1)

    sib = dev(x, y, 1 - c)
    sends = []
    core_cp = [
        rc(grads.at[0, 2 * (1 - c) + 1 - y], g_other.at[1], CORE, CORE, sib),
        rc(grads.at[0, 2 * (1 - c) + y], g_mine.at[1], CORE + 1, CORE + 1, sib),
    ]
    for cp in core_cp:
        cp.start()
    raw_cp = []
    for n, k in enumerate(ORDER):
        cols = pl.ds(pl.multiple_of(xo(k) * T, T), T)
        for h in range(2):
            cc = c if h == 0 else 1 - c
            cp = rc(
                grads.at[0, 2 * cc + 1 - y, :, cols],
                g_mine.at[2 + h, :, cols],
                RAW + 2 * n + h,
                RAW + 2 * n + h,
                dev(x, 1 - y, cc),
            )
            cp.start()
            raw_cp.append(cp)
    sends += core_cp + raw_cp

    rows_i = lax.broadcasted_iota(jnp.int32, (T, T), 0)
    cols_i = lax.broadcasted_iota(jnp.int32, (T, T), 1)
    above = rows_i < cols_i
    below = rows_i > cols_i
    on = rows_i == cols_i

    def diag_of(t):
        return jnp.sum(jnp.where(on, t, 0.0), axis=0, keepdims=True)

    def stats(which, g):
        def pack(s, top, bot):
            for n, (i, j) in enumerate(OFF_TILES):
                if i < 2:
                    t = top[i * T : (i + 1) * T, j * T : (j + 1) * T]
                else:
                    t = bot[(i - 2) * T : (i - 1) * T, (j - 2) * T : (j - 1) * T]
                packed[which, s, tile_of(n), :] = t.astype(BF16)
            d = [
                top[0:T, 0:T],
                top[T : 2 * T, T : 2 * T],
                bot[0:T, 0:T],
                bot[T : 2 * T, T : 2 * T],
            ]
            packed[which, s, tile_of(6), :] = jnp.where(above, d[0], d[1]).astype(BF16)
            packed[which, s, tile_of(7), :] = jnp.where(above, d[2], d[3]).astype(BF16)
            dg_out[which, s] = jnp.zeros((8, T), F32)
            for n in range(4):
                dg_out[which, s, n : n + 1, :] = diag_of(d[n])

        for h in range(2):
            tr[h] = g[h].T
        h2 = BS // 2
        top = dot(g[0, :h2, :], tr[0]) + dot(g[1, :h2, :], tr[1])
        bot = dot(g[0, h2:, :], tr[0, :, h2:]) + dot(g[1, h2:, :], tr[1, :, h2:])
        pack(0, top, bot)
        top = dot(tr[0, :h2, :], g[0]) + dot(tr[1, :h2, :], g[1])
        bot = dot(tr[0, h2:, :], g[0, :, h2:]) + dot(tr[1, h2:, :], g[1, :, h2:])
        pack(1, top, bot)

    def stat_cp(which, s):
        xt = 2 * s + c
        k = lax.rem(xt - x + 4, 4)
        slot = jnp.maximum(k - 1, 0)
        return k, rc(
            packed.at[which, s],
            got.at[which, slot],
            STAT + 2 * which + s,
            STAT + 3 * which + slot,
            dev(xt, y, c),
        )

    def dg_cp(which, s):
        yt = 1 - y if which == 0 else y
        return rc(
            dg_out.at[which, s],
            dg_in.at[2 * x + y],
            DG + 2 * which + s,
            DG + 2 * x + y,
            dev(2 * s + c, yt, c),
        )

    def stat_sends(which, act):
        for s in range(2):
            k, cp = stat_cp(which, s)
            pl.when(k != 0)(lambda cp=cp: act(cp))
            cp2 = dg_cp(which, s)
            if which == 0:
                act(cp2)
            else:
                pl.when(k != 0)(lambda cp2=cp2: act(cp2))

    loads[0].wait()
    core_cp[0].wait_recv()
    stats(0, g_other)
    stat_sends(0, lambda cp: cp.start())
    loads[1].wait()
    core_cp[1].wait_recv()
    stats(1, g_mine)
    stat_sends(1, lambda cp: cp.start())

    def raw_sum(n):
        cols = pl.ds(pl.multiple_of(xo(ORDER[n]) * T, T), T)
        raw_cp[2 * n].wait_recv()
        raw_cp[2 * n + 1].wait_recv()
        t = g_mine[0, :, cols].astype(F32) + g_mine[1, :, cols].astype(F32)
        return t + (g_mine[2, :, cols].astype(F32) + g_mine[3, :, cols].astype(F32))

    grd_cp = []

    def grad_chunk(n):
        k = ORDER[n]
        g_send[k - 1] = raw_sum(n)
        cp = rc(g_send.at[k - 1], g_recv.at[k - 1], GRD + k - 1, GRD + k - 1, dev(xo(k), y, c))
        cp.start()
        grd_cp.append(cp)

    def wait_stats(which):
        for slot in range(3):
            rc(
                packed.at[which, 0],
                got.at[which, slot],
                STAT,
                STAT + 3 * which + slot,
                dev(x, 1 - y, c),
            ).wait_recv()

    def stat_tile(which, n):
        t = packed[which, keep, tile_of(n), :].astype(F32)
        for slot in range(3):
            t = t + got[which, slot, tile_of(n), :].astype(F32)
        return t

    y_cp = rc(y_out, y_in, SUMY, SUMY, dev(x, 1 - y, c))

    grad_chunk(0)

    @pl.when(even)
    def _():
        wait_stats(0)
        for n in range(8):
            y_out[tile_of(n), :] = stat_tile(0, n).astype(BF16)
        y_cp.start()

    grad_chunk(1)

    my_piece = 4 * c + 2 * y + keep

    def ring_cp(row, k):
        yr = y if row == 0 else 1 - y
        ref = pieces.at[4 * c + 2 * yr + keep]
        return rc(ref, ref, AGS + 4 * row + k - 1, AGR + 2 * row + keep, dev(xo(k), y, c))

    def ycopy():
        ref = pieces.at[my_piece]
        return rc(ref, ref, AGS + 3, AGR + 2 + keep, dev(x, 1 - y, c))

    @pl.when(even)
    def _():
        wait_stats(1)
        y_cp.wait_recv()
        dsum = dg_out[1, keep]
        for sender in range(8):

            @pl.when(sender != 2 * x + y)
            def _():
                rc(
                    dg_out.at[0, 0], dg_in.at[sender], DG, DG + sender, dev(x, 1 - y, c)
                ).wait_recv()

        for sender in range(8):
            dsum = dsum + jnp.where(sender != 2 * x + y, dg_in[sender], 0.0)
        dsum = dsum * (1.0 / N_DP) + 0.0001

        def full_tile(n):
            return (stat_tile(1, n) + y_in[tile_of(n), :].astype(F32)) * (1.0 / N_DP)

        off_sq = jnp.zeros((T, T), F32)
        for n, (i, j) in enumerate(OFF_TILES):
            t = full_tile(n)
            off_sq = off_sq + t * t
            mat[tile_of(i), tile_of(j)] = t
            mat[tile_of(j), tile_of(i)] = t.T
        for n, (i, j) in ((6, (0, 1)), (7, (2, 3))):
            t = full_tile(n)
            tt = t.T
            d0, d1 = dsum[i : i + 1, :], dsum[j : j + 1, :]
            off_sq = off_sq + jnp.where(on, 0.0, t * t)
            mat[tile_of(i), tile_of(i)] = jnp.where(above, t, jnp.where(below, tt, d0))
            mat[tile_of(j), tile_of(j)] = jnp.where(below, t, jnp.where(above, tt, d1))
        total = 2.0 * jnp.sum(off_sq) + jnp.sum(
            jnp.where(lax.broadcasted_iota(jnp.int32, (8, T), 0) < 4, dsum * dsum, 0.0)
        )
        inv = 1.0 / jnp.sqrt(jnp.full((1, 1), total, F32))
        mat[...] = mat[...] * inv
        mat_b[...] = mat[...].astype(BF16)
        yy[...] = mat[...] * -0.25
        yy_b[...] = yy[...].astype(BF16)
        scale = 1.25
        for _step in range(2):
            ee[...] = (dot(mat_b[...], mat_b[...]) - 10.0 * mat[...]) * (1.0 / 16.0)
            ee_b[...] = ee[...].astype(BF16)
            ee_b[...] = (3.125 * ee[...] + dot(ee_b[...], ee_b[...])).astype(BF16)
            mat[...] = (625.0 / 256.0) * mat[...] + dot(mat_b[...], ee_b[...])
            mat_b[...] = mat[...].astype(BF16)
            yy[...] = (
                1.25 * yy[...] - (scale / 4.0) * mat[...] - 0.25 * dot(yy_b[...], mat_b[...])
            )
            yy_b[...] = yy[...].astype(BF16)
            scale = scale * 1.25
        for n, (i, j) in enumerate(OFF_TILES):
            pieces[my_piece, tile_of(n), :] = yy[tile_of(i), tile_of(j)].astype(BF16)
        for n, (i, j) in ((6, (0, 1)), (7, (2, 3))):
            pieces[my_piece, tile_of(n), :] = jnp.where(
                above, yy[tile_of(i), tile_of(i)], yy[tile_of(j), tile_of(j)]
            ).astype(BF16)
        ds = [diag_of(yy[tile_of(i), tile_of(i)]) + scale for i in range(4)]
        pieces[my_piece, PIECE : PIECE + DIAG, :] = jnp.concatenate(
            ds + [jnp.zeros((DIAG - 4, T), F32)], axis=0
        ).astype(BF16)
        ycopy().start()
        for k in (1, 3, 2):
            ring_cp(0, k).start()

    grad_chunk(2)

    def piece_at(row, s):
        yr = y if row == 0 else 1 - y
        return pieces.at[4 * c + 2 * yr + s]

    def other_piece_at(row, s):
        yr = y if row == 0 else 1 - y
        return pieces.at[4 * (1 - c) + 2 * yr + s]

    def sib_cp(row, s):
        return rc(piece_at(row, s), piece_at(row, s), SIB + 2 * row + s, SIB + 2 * row + s, sib)

    def ag_wait(row, s):
        ref = piece_at(row, s)
        rc(ref, ref, AGR, AGR + 2 * row + s, dev(x, 1 - y, c)).wait_recv()

    own = raw_sum(3)
    for k in (2, 1, 3):
        grd_cp[(2, 1, 3).index(k)].wait_recv()
        own = own + g_recv[k - 1]
    gm_loc[...] = own * (1.0 / N_DP)
    my_cols = pl.ds(pl.multiple_of(x * T, T), T)

    def gm_cp(k):
        to = lax.rem(me + k, N_DP)
        r = pl.ds(pl.multiple_of(to * ROWS, ROWS), ROWS)
        return rc(gm_loc.at[r], gm_rows.at[blk, :, my_cols], GMX + k, GMX + k, (to, col))

    def sc_cp(k):
        to = lax.rem(me + k, N_DP)
        r = pl.ds(pl.multiple_of(to * ROWS, ROWS), ROWS)
        return rc(sc_loc.at[r], sc_rows.at[blk, :, my_cols], SCX + k, SCX + k, (to, col))

    my_rows = pl.ds(pl.multiple_of(me * ROWS, ROWS), ROWS)
    for k in range(1, N_DP):
        gm_cp(k).start()
    loads[2].wait()
    sc_loc[...] = dot(left_v[...], gm_loc[...].astype(BF16)).astype(BF16)
    for k in range(1, N_DP):
        sc_cp(k).start()
    gm_rows[blk, :, my_cols] = gm_loc[my_rows, :]
    sc_rows[blk, :, my_cols] = sc_loc[my_rows, :]

    @pl.when(even)
    def _():
        sib_cp(0, keep).start()
        ag_wait(1, keep)
        for k in (1, 3, 2):
            ring_cp(1, k).start()
        sib_cp(1, keep).start()
        ag_wait(0, 1 - keep)
        sib_cp(0, 1 - keep).start()

    @pl.when(jnp.logical_not(even))
    def _():
        for s in range(2):
            ag_wait(0, s)
            sib_cp(0, s).start()

    for k in range(1, N_DP):
        gm_cp(k).wait_recv()
    g = gm_rows[...]
    first = 0.9 * m1[...] + 0.1 * g
    second = 0.95 * m2[...] + 0.05 * g * g
    m1n[...] = first
    m2n[...] = second
    adam = first / (jnp.sqrt(second) + 1e-08)
    adam_sq = jnp.sum(adam * adam)
    for b in range(4):
        loads[3 + b].wait()
    for k in range(1, N_DP):
        sc_cp(k).wait_recv()
    pre_sq = jnp.zeros((ROWS, BS), F32)
    for b in range(4):
        p = dot(sc_rows[b], right_v[b])
        precond[b] = p
        pre_sq = pre_sq + p * p
    pre_sq = jnp.sum(pre_sq)
    row8 = lax.broadcasted_iota(jnp.int32, (8, T), 0)
    mine = jnp.where(row8 == 0, adam_sq, jnp.where(row8 == 1, pre_sq, 0.0))
    s1_out[...] = mine

    def s1_cp(k):
        return rc(s1_out, s1_in.at[k], SC1 + k, SC1 + k, (lax.rem(me + k, N_DP), col))

    def s2_cp(k):
        return rc(s2_out, s2_in.at[k], SC2 + k, SC2 + k, (me, lax.rem(col + k, n_mp)))

    for k in range(1, N_DP):
        s1_cp(k).start()
    for k in range(1, N_DP):
        s1_cp(k).wait_recv()
    for k in range(1, N_DP):
        mine = mine + s1_in[k]
    s2_out[...] = mine
    for k in range(1, n_mp):
        s2_cp(k).start()

    @pl.when(even)
    def _():
        ag_wait(1, 1 - keep)
        sib_cp(1, 1 - keep).start()

    @pl.when(jnp.logical_not(even))
    def _():
        for s in range(2):
            ag_wait(1, s)
            sib_cp(1, s).start()

    for k in range(1, n_mp):
        s2_cp(k).wait_recv()
    for k in range(1, n_mp):
        mine = mine + s2_in[k]
    ratio = jnp.sqrt(mine[0:1, :]) / jnp.sqrt(mine[1:2, :] + 1e-06)
    for b in range(4):
        for n in range(4):
            update[b, :, tile_of(n)] = precond[b, :, tile_of(n)] * ratio

    for row in range(2):
        for s in range(2):
            ref = other_piece_at(row, s)
            rc(ref, ref, SIB, SIB + 2 * row + s, sib).wait_recv()

    first_id, second_id, n_mine = jnp.int32(0), jnp.int32(0), jnp.int32(0)
    for i in range(8):
        hit = owners[i, 0] == me
        first_id = jnp.where(hit & (n_mine == 0), i, first_id)
        second_id = jnp.where(hit & (n_mine == 1), i, second_id)
        n_mine = n_mine + jnp.where(hit, 1, 0)
    for slot, idx in ((0, first_id), (1, second_id)):
        filled = n_mine > slot

        def piece_tile(n):
            return jnp.where(filled, pieces[idx, tile_of(n), :].astype(F32), 0.0)

        for n, (i, j) in enumerate(OFF_TILES):
            t = piece_tile(n)
            roots_new[slot, tile_of(i), tile_of(j)] = t.astype(BF16)
            roots_new[slot, tile_of(j), tile_of(i)] = t.T.astype(BF16)
        dg = jnp.where(filled, pieces[idx, PIECE : PIECE + DIAG, :].astype(F32), 0.0)
        for n, (i, j) in ((6, (0, 1)), (7, (2, 3))):
            t = piece_tile(n)
            tt = t.T
            d0, d1 = dg[i : i + 1, :], dg[j : j + 1, :]
            roots_new[slot, tile_of(i), tile_of(i)] = jnp.where(
                above, t, jnp.where(below, tt, d0)
            ).astype(BF16)
            roots_new[slot, tile_of(j), tile_of(j)] = jnp.where(
                below, t, jnp.where(above, tt, d1)
            ).astype(BF16)

    for cp in sends + grd_cp:
        cp.wait_send()
    stat_sends(0, lambda cp: cp.wait_send())
    stat_sends(1, lambda cp: cp.wait_send())

    @pl.when(even)
    def _():
        y_cp.wait_send()
        ycopy().wait_send()
        for row in range(2):
            for k in (1, 3, 2):
                ring_cp(row, k).wait_send()

    for row in range(2):
        for s in range(2):
            sib_cp(row, s).wait_send()
    for k in range(1, N_DP):
        gm_cp(k).wait_send()
        sc_cp(k).wait_send()
        s1_cp(k).wait_send()
    for k in range(1, n_mp):
        s2_cp(k).wait_send()


def per_device(grads, owners, roots_prev, moment_first, moment_second):
    n_mp = lax.axis_size("mp")
    any_spec = pl.BlockSpec(memory_space=pl.ANY)
    vmem = pl.BlockSpec(memory_space=pltpu.VMEM)
    small = jax.ShapeDtypeStruct((4, ROWS, BS), F32)

    def body(*refs):
        kernel(n_mp, *refs)

    update, m1n, m2n, roots_new = pl.pallas_call(
        body,
        out_shape=(small, small, small, jax.ShapeDtypeStruct((2, BS, BS), BF16)),
        in_specs=[pl.BlockSpec(memory_space=pltpu.SMEM), any_spec, any_spec, vmem, vmem],
        out_specs=(vmem, vmem, vmem, vmem),
        scratch_shapes=[
            pltpu.VMEM((4, BS, BS), BF16),
            pltpu.VMEM((2, BS, BS), BF16),
            pltpu.VMEM((BS, BS), BF16),
            pltpu.VMEM((4, BS, BS), BF16),
            pltpu.VMEM((2, BS, BS), BF16),
            pltpu.VMEM((2, 2, PIECE, T), BF16),
            pltpu.VMEM((2, 3, PIECE, T), BF16),
            pltpu.VMEM((PIECE, T), BF16),
            pltpu.VMEM((PIECE, T), BF16),
            pltpu.VMEM((2, 2, 8, T), F32),
            pltpu.VMEM((8, 8, T), F32),
            pltpu.VMEM((3, BS, T), F32),
            pltpu.VMEM((3, BS, T), F32),
            pltpu.VMEM((BS, T), F32),
            pltpu.VMEM((BS, T), BF16),
            pltpu.VMEM((4, ROWS, BS), F32),
            pltpu.VMEM((4, ROWS, BS), BF16),
            pltpu.VMEM((8, PIECE + DIAG, T), BF16),
            pltpu.VMEM((BS, BS), F32),
            pltpu.VMEM((BS, BS), BF16),
            pltpu.VMEM((BS, BS), F32),
            pltpu.VMEM((BS, BS), BF16),
            pltpu.VMEM((BS, BS), F32),
            pltpu.VMEM((BS, BS), BF16),
            pltpu.VMEM((4, ROWS, BS), F32),
            pltpu.VMEM((8, T), F32),
            pltpu.VMEM((N_DP, 8, T), F32),
            pltpu.VMEM((8, T), F32),
            pltpu.VMEM((max(n_mp, 2), 8, T), F32),
            pltpu.SemaphoreType.DMA((N_SEM,)),
            pltpu.SemaphoreType.DMA((N_SEM,)),
            pltpu.SemaphoreType.DMA((LOC,)),
        ],
        compiler_params=pltpu.CompilerParams(
            collective_id=0, has_side_effects=True, vmem_limit_bytes=48 * 2**20
        ),
        name="shampoo",
    )(owners, grads, roots_prev, moment_first, moment_second)
    return update, m1n, m2n, roots_new[None, None]


def solution(mesh):
    return jax.shard_map(
        per_device,
        mesh=mesh,
        in_specs=(
            P("dp", "mp", None, None),
            P("mp", None),
            P("mp", None, None, None),
            P("mp", "dp", None),
            P("mp", "dp", None),
        ),
        out_specs=(
            P("mp", "dp", None),
            P("mp", "dp", None),
            P("mp", "dp", None),
            P("dp", "mp", None, None, None),
        ),
        check_vma=False,
    )
```

```python
import jax
import jax.numpy as jnp
from jax import lax
from jax.experimental import pallas as pl
from jax.experimental.pallas import tpu as pltpu
from jax.sharding import PartitionSpec as P

MESH = pl.DeviceIdType.MESH
F32 = jnp.float32
BF16 = jnp.bfloat16
BS = 512
T = 128
N_DP = 16
ROWS = BS // N_DP
PIECE = 8 * T
DIAG = 16
OFF_TILES = ((0, 1), (0, 2), (0, 3), (1, 2), (1, 3), (2, 3))
ORDER = (2, 1, 3, 0)

CORE = 0
RAW = 2
STAT = 10
SUMY = 16
DG = 17
GRD = 25
GMX = 28
SCX = 44
AGR = 60
SIB = 64
SC1 = 68
SC2 = 84
AGS = 100
N_SEM = 108
LOC = 9


def dot(a, b):
    return jnp.dot(a, b, preferred_element_type=F32)


def tile_of(t):
    return pl.ds(t * T, T)


def kernel(
    n_mp,
    owners,
    grads,
    roots,
    m1_hbm,
    m2_hbm,
    update,
    m1n,
    m2n,
    roots_new,
    g_mine,
    g_other,
    left_v,
    right_v,
    tr,
    packed,
    got,
    y_out,
    y_in,
    dg_out,
    dg_in,
    g_send,
    g_recv,
    gm_loc,
    sc_loc,
    gm_rows,
    sc_rows,
    pieces,
    mat,
    mat_b,
    yy,
    yy_b,
    ee,
    ee_b,
    precond,
    s1_out,
    s1_in,
    s2_out,
    s2_in,
    m1,
    m2,
    ss,
    rs,
    ls,
):
    me = lax.axis_index("dp")
    col = lax.axis_index("mp")
    x, y, c = me // 4, (me // 2) % 2, me % 2
    even = (x % 2) == c
    keep = x // 2
    blk = 2 * c + y

    def dev(xx, yv, cc):
        return (xx * 4 + yv * 2 + cc, col)

    def xo(k):
        return lax.rem(x + k, 4)

    def rc(src, dst, i_send, i_recv, where):
        return pltpu.make_async_remote_copy(
            src_ref=src,
            dst_ref=dst,
            send_sem=ss.at[i_send],
            recv_sem=rs.at[i_recv],
            device_id=where,
            device_id_type=MESH,
        )

    barrier = pltpu.get_barrier_semaphore()
    for k in range(1, N_DP):
        pl.semaphore_signal(
            barrier, inc=1, device_id=(lax.rem(me + k, N_DP), col), device_id_type=MESH
        )
    for k in range(1, n_mp):
        pl.semaphore_signal(
            barrier, inc=1, device_id=(me, lax.rem(col + k, n_mp)), device_id_type=MESH
        )

    loads = [
        pltpu.make_async_copy(grads.at[0, 2 * c + 1 - y], g_other.at[0], ls.at[0]),
        pltpu.make_async_copy(grads.at[0, 2 * c + y], g_mine.at[0], ls.at[1]),
        pltpu.make_async_copy(roots.at[blk, 0], left_v, ls.at[2]),
    ] + [
        pltpu.make_async_copy(roots.at[b, 1], right_v.at[b], ls.at[3 + b]) for b in range(4)
    ] + [
        pltpu.make_async_copy(m1_hbm, m1, ls.at[7]),
        pltpu.make_async_copy(m2_hbm, m2, ls.at[8]),
    ]
    for cp in loads:
        cp.start()
    pl.semaphore_wait(barrier, N_DP - 1 + n_mp - 1)

    sib = dev(x, y, 1 - c)
    sends = []
    core_cp = [
        rc(grads.at[0, 2 * (1 - c) + 1 - y], g_other.at[1], CORE, CORE, sib),
        rc(grads.at[0, 2 * (1 - c) + y], g_mine.at[1], CORE + 1, CORE + 1, sib),
    ]
    for cp in core_cp:
        cp.start()
    raw_cp = []
    for n, k in enumerate(ORDER):
        cols = pl.ds(pl.multiple_of(xo(k) * T, T), T)
        for h in range(2):
            cc = c if h == 0 else 1 - c
            cp = rc(
                grads.at[0, 2 * cc + 1 - y, :, cols],
                g_mine.at[2 + h, :, cols],
                RAW + 2 * n + h,
                RAW + 2 * n + h,
                dev(x, 1 - y, cc),
            )
            cp.start()
            raw_cp.append(cp)
    sends += core_cp + raw_cp

    rows_i = lax.broadcasted_iota(jnp.int32, (T, T), 0)
    cols_i = lax.broadcasted_iota(jnp.int32, (T, T), 1)
    above = rows_i < cols_i
    below = rows_i > cols_i
    on = rows_i == cols_i

    def diag_of(t):
        return jnp.sum(jnp.where(on, t, 0.0), axis=0, keepdims=True)

    def stats(which, g):
        def pack(s, top, bot):
            for n, (i, j) in enumerate(OFF_TILES):
                if i < 2:
                    t = top[i * T : (i + 1) * T, j * T : (j + 1) * T]
                else:
                    t = bot[(i - 2) * T : (i - 1) * T, (j - 2) * T : (j - 1) * T]
                packed[which, s, tile_of(n), :] = t.astype(BF16)
            d = [
                top[0:T, 0:T],
                top[T : 2 * T, T : 2 * T],
                bot[0:T, 0:T],
                bot[T : 2 * T, T : 2 * T],
            ]
            packed[which, s, tile_of(6), :] = jnp.where(above, d[0], d[1]).astype(BF16)
            packed[which, s, tile_of(7), :] = jnp.where(above, d[2], d[3]).astype(BF16)
            dg_out[which, s] = jnp.zeros((8, T), F32)
            for n in range(4):
                dg_out[which, s, n : n + 1, :] = diag_of(d[n])

        for h in range(2):
            tr[h] = g[h].T
        h2 = BS // 2
        top = dot(g[0, :h2, :], tr[0]) + dot(g[1, :h2, :], tr[1])
        bot = dot(g[0, h2:, :], tr[0, :, h2:]) + dot(g[1, h2:, :], tr[1, :, h2:])
        pack(0, top, bot)
        top = dot(tr[0, :h2, :], g[0]) + dot(tr[1, :h2, :], g[1])
        bot = dot(tr[0, h2:, :], g[0, :, h2:]) + dot(tr[1, h2:, :], g[1, :, h2:])
        pack(1, top, bot)

    def stat_cp(which, s):
        xt = 2 * s + c
        k = lax.rem(xt - x + 4, 4)
        slot = jnp.maximum(k - 1, 0)
        return k, rc(
            packed.at[which, s],
            got.at[which, slot],
            STAT + 2 * which + s,
            STAT + 3 * which + slot,
            dev(xt, y, c),
        )

    def dg_cp(which, s):
        yt = 1 - y if which == 0 else y
        return rc(
            dg_out.at[which, s],
            dg_in.at[2 * x + y],
            DG + 2 * which + s,
            DG + 2 * x + y,
            dev(2 * s + c, yt, c),
        )

    def stat_sends(which, act):
        for s in range(2):
            k, cp = stat_cp(which, s)
            pl.when(k != 0)(lambda cp=cp: act(cp))
            cp2 = dg_cp(which, s)
            if which == 0:
                act(cp2)
            else:
                pl.when(k != 0)(lambda cp2=cp2: act(cp2))

    loads[0].wait()
    core_cp[0].wait_recv()
    stats(0, g_other)
    stat_sends(0, lambda cp: cp.start())
    loads[1].wait()
    core_cp[1].wait_recv()
    stats(1, g_mine)
    stat_sends(1, lambda cp: cp.start())

    def raw_sum(n):
        cols = pl.ds(pl.multiple_of(xo(ORDER[n]) * T, T), T)
        raw_cp[2 * n].wait_recv()
        raw_cp[2 * n + 1].wait_recv()
        t = g_mine[0, :, cols].astype(F32) + g_mine[1, :, cols].astype(F32)
        return t + (g_mine[2, :, cols].astype(F32) + g_mine[3, :, cols].astype(F32))

    grd_cp = []

    def grad_chunk(n):
        k = ORDER[n]
        g_send[k - 1] = raw_sum(n)
        cp = rc(g_send.at[k - 1], g_recv.at[k - 1], GRD + k - 1, GRD + k - 1, dev(xo(k), y, c))
        cp.start()
        grd_cp.append(cp)

    def wait_stats(which):
        for slot in range(3):
            rc(
                packed.at[which, 0],
                got.at[which, slot],
                STAT,
                STAT + 3 * which + slot,
                dev(x, 1 - y, c),
            ).wait_recv()

    def stat_tile(which, n):
        t = packed[which, keep, tile_of(n), :].astype(F32)
        for slot in range(3):
            t = t + got[which, slot, tile_of(n), :].astype(F32)
        return t

    y_cp = rc(y_out, y_in, SUMY, SUMY, dev(x, 1 - y, c))

    grad_chunk(0)

    @pl.when(even)
    def _():
        wait_stats(0)
        for n in range(8):
            y_out[tile_of(n), :] = stat_tile(0, n).astype(BF16)
        y_cp.start()

    grad_chunk(1)

    my_piece = 4 * c + 2 * y + keep

    def ring_cp(row, k):
        yr = y if row == 0 else 1 - y
        ref = pieces.at[4 * c + 2 * yr + keep]
        return rc(ref, ref, AGS + 4 * row + k - 1, AGR + 2 * row + keep, dev(xo(k), y, c))

    def ycopy():
        ref = pieces.at[my_piece]
        return rc(ref, ref, AGS + 3, AGR + 2 + keep, dev(x, 1 - y, c))

    grad_chunk(2)

    def piece_at(row, s):
        yr = y if row == 0 else 1 - y
        return pieces.at[4 * c + 2 * yr + s]

    def other_piece_at(row, s):
        yr = y if row == 0 else 1 - y
        return pieces.at[4 * (1 - c) + 2 * yr + s]

    def sib_cp(row, s):
        return rc(piece_at(row, s), piece_at(row, s), SIB + 2 * row + s, SIB + 2 * row + s, sib)

    def ag_wait(row, s):
        ref = piece_at(row, s)
        rc(ref, ref, AGR, AGR + 2 * row + s, dev(x, 1 - y, c)).wait_recv()

    own = raw_sum(3)
    for k in (2, 1, 3):
        grd_cp[(2, 1, 3).index(k)].wait_recv()
        own = own + g_recv[k - 1]
    gm_loc[...] = own * (1.0 / N_DP)
    my_cols = pl.ds(pl.multiple_of(x * T, T), T)

    def gm_cp(k):
        to = lax.rem(me + k, N_DP)
        r = pl.ds(pl.multiple_of(to * ROWS, ROWS), ROWS)
        return rc(gm_loc.at[r], gm_rows.at[blk, :, my_cols], GMX + k, GMX + k, (to, col))

    def sc_cp(k):
        to = lax.rem(me + k, N_DP)
        r = pl.ds(pl.multiple_of(to * ROWS, ROWS), ROWS)
        return rc(sc_loc.at[r], sc_rows.at[blk, :, my_cols], SCX + k, SCX + k, (to, col))

    my_rows = pl.ds(pl.multiple_of(me * ROWS, ROWS), ROWS)
    for k in range(1, N_DP):
        gm_cp(k).start()
    loads[2].wait()
    sc_loc[...] = dot(left_v[...], gm_loc[...].astype(BF16)).astype(BF16)
    for k in range(1, N_DP):
        sc_cp(k).start()
    gm_rows[blk, :, my_cols] = gm_loc[my_rows, :]
    sc_rows[blk, :, my_cols] = sc_loc[my_rows, :]

    @pl.when(even)
    def _():
        y_cp.wait_recv()
        wait_stats(1)
        dsum = dg_out[1, keep]
        for sender in range(8):

            @pl.when(sender != 2 * x + y)
            def _():
                rc(
                    dg_out.at[0, 0], dg_in.at[sender], DG, DG + sender, dev(x, 1 - y, c)
                ).wait_recv()

        for sender in range(8):
            dsum = dsum + jnp.where(sender != 2 * x + y, dg_in[sender], 0.0)
        dsum = dsum * (1.0 / N_DP) + 0.0001

        def full_tile(n):
            return (stat_tile(1, n) + y_in[tile_of(n), :].astype(F32)) * (1.0 / N_DP)

        off_sq = jnp.zeros((T, T), F32)
        for n, (i, j) in enumerate(OFF_TILES):
            t = full_tile(n)
            off_sq = off_sq + t * t
            mat[tile_of(i), tile_of(j)] = t
            mat[tile_of(j), tile_of(i)] = t.T
        for n, (i, j) in ((6, (0, 1)), (7, (2, 3))):
            t = full_tile(n)
            tt = t.T
            d0, d1 = dsum[i : i + 1, :], dsum[j : j + 1, :]
            off_sq = off_sq + jnp.where(on, 0.0, t * t)
            mat[tile_of(i), tile_of(i)] = jnp.where(above, t, jnp.where(below, tt, d0))
            mat[tile_of(j), tile_of(j)] = jnp.where(below, t, jnp.where(above, tt, d1))
        total = 2.0 * jnp.sum(off_sq) + jnp.sum(
            jnp.where(lax.broadcasted_iota(jnp.int32, (8, T), 0) < 4, dsum * dsum, 0.0)
        )
        inv = 1.0 / jnp.sqrt(jnp.full((1, 1), total, F32))
        mat[...] = mat[...] * inv
        mat_b[...] = mat[...].astype(BF16)
        yy[...] = mat[...] * -0.25
        yy_b[...] = yy[...].astype(BF16)
        scale = 1.25
        for _step in range(2):
            ee[...] = (dot(mat_b[...], mat_b[...]) - 10.0 * mat[...]) * (1.0 / 16.0)
            ee_b[...] = ee[...].astype(BF16)
            ee_b[...] = (3.125 * ee[...] + dot(ee_b[...], ee_b[...])).astype(BF16)
            mat[...] = (625.0 / 256.0) * mat[...] + dot(mat_b[...], ee_b[...])
            mat_b[...] = mat[...].astype(BF16)
            yy[...] = (
                1.25 * yy[...] - (scale / 4.0) * mat[...] - 0.25 * dot(yy_b[...], mat_b[...])
            )
            yy_b[...] = yy[...].astype(BF16)
            scale = scale * 1.25
        for n, (i, j) in enumerate(OFF_TILES):
            pieces[my_piece, tile_of(n), :] = yy[tile_of(i), tile_of(j)].astype(BF16)
        for n, (i, j) in ((6, (0, 1)), (7, (2, 3))):
            pieces[my_piece, tile_of(n), :] = jnp.where(
                above, yy[tile_of(i), tile_of(i)], yy[tile_of(j), tile_of(j)]
            ).astype(BF16)
        ds = [diag_of(yy[tile_of(i), tile_of(i)]) + scale for i in range(4)]
        pieces[my_piece, PIECE : PIECE + DIAG, :] = jnp.concatenate(
            ds + [jnp.zeros((DIAG - 4, T), F32)], axis=0
        ).astype(BF16)
        ycopy().start()
        for k in (1, 3, 2):
            ring_cp(0, k).start()

    for k in range(1, N_DP):
        gm_cp(k).wait_recv()
    loads[7].wait()
    loads[8].wait()
    g = gm_rows[...]
    first = 0.9 * m1[...] + 0.1 * g
    second = 0.95 * m2[...] + 0.05 * g * g
    m1n[...] = first
    m2n[...] = second
    adam = first / (jnp.sqrt(second) + 1e-08)
    adam_sq = jnp.sum(adam * adam)
    for b in range(4):
        loads[3 + b].wait()
    for k in range(1, N_DP):
        sc_cp(k).wait_recv()
    pre_sq = jnp.zeros((ROWS, BS), F32)
    for b in range(4):
        p = dot(sc_rows[b], right_v[b])
        precond[b] = p
        pre_sq = pre_sq + p * p
    pre_sq = jnp.sum(pre_sq)
    row8 = lax.broadcasted_iota(jnp.int32, (8, T), 0)
    mine = jnp.where(row8 == 0, adam_sq, jnp.where(row8 == 1, pre_sq, 0.0))
    s1_out[...] = mine

    def s1_cp(k):
        return rc(s1_out, s1_in.at[k], SC1 + k, SC1 + k, (lax.rem(me + k, N_DP), col))

    def s2_cp(k):
        return rc(s2_out, s2_in.at[k], SC2 + k, SC2 + k, (me, lax.rem(col + k, n_mp)))

    for k in range(1, N_DP):
        s1_cp(k).start()

    @pl.when(even)
    def _():
        sib_cp(0, keep).start()
        ag_wait(1, keep)
        for k in (1, 3, 2):
            ring_cp(1, k).start()
        sib_cp(1, keep).start()

    @pl.when(jnp.logical_not(even))
    def _():
        for s in range(2):
            ag_wait(0, s)
            sib_cp(0, s).start()

    for k in range(1, N_DP):
        s1_cp(k).wait_recv()
    for k in range(1, N_DP):
        mine = mine + s1_in[k]
    s2_out[...] = mine
    for k in range(1, n_mp):
        s2_cp(k).start()

    @pl.when(even)
    def _():
        for row in range(2):
            ag_wait(row, 1 - keep)
            sib_cp(row, 1 - keep).start()

    @pl.when(jnp.logical_not(even))
    def _():
        for s in range(2):
            ag_wait(1, s)
            sib_cp(1, s).start()

    for row in range(2):
        for s in range(2):
            ref = other_piece_at(row, s)
            rc(ref, ref, SIB, SIB + 2 * row + s, sib).wait_recv()

    first_id, second_id, n_mine = jnp.int32(0), jnp.int32(0), jnp.int32(0)
    for i in range(8):
        hit = owners[i, 0] == me
        first_id = jnp.where(hit & (n_mine == 0), i, first_id)
        second_id = jnp.where(hit & (n_mine == 1), i, second_id)
        n_mine = n_mine + jnp.where(hit, 1, 0)
    for slot, idx in ((0, first_id), (1, second_id)):
        filled = n_mine > slot

        def piece_tile(n):
            return jnp.where(filled, pieces[idx, tile_of(n), :].astype(F32), 0.0)

        for n, (i, j) in enumerate(OFF_TILES):
            t = piece_tile(n)
            roots_new[slot, tile_of(i), tile_of(j)] = t.astype(BF16)
            roots_new[slot, tile_of(j), tile_of(i)] = t.T.astype(BF16)
        dg = jnp.where(filled, pieces[idx, PIECE : PIECE + DIAG, :].astype(F32), 0.0)
        for n, (i, j) in ((6, (0, 1)), (7, (2, 3))):
            t = piece_tile(n)
            tt = t.T
            d0, d1 = dg[i : i + 1, :], dg[j : j + 1, :]
            roots_new[slot, tile_of(i), tile_of(i)] = jnp.where(
                above, t, jnp.where(below, tt, d0)
            ).astype(BF16)
            roots_new[slot, tile_of(j), tile_of(j)] = jnp.where(
                below, t, jnp.where(above, tt, d1)
            ).astype(BF16)

    for k in range(1, n_mp):
        s2_cp(k).wait_recv()
    for k in range(1, n_mp):
        mine = mine + s2_in[k]
    ratio = jnp.sqrt(mine[0:1, :]) / jnp.sqrt(mine[1:2, :] + 1e-06)
    for b in range(4):
        for n in range(4):
            update[b, :, tile_of(n)] = precond[b, :, tile_of(n)] * ratio

    for cp in sends + grd_cp:
        cp.wait_send()
    stat_sends(0, lambda cp: cp.wait_send())
    stat_sends(1, lambda cp: cp.wait_send())

    @pl.when(even)
    def _():
        y_cp.wait_send()
        ycopy().wait_send()
        for row in range(2):
            for k in (1, 3, 2):
                ring_cp(row, k).wait_send()

    for row in range(2):
        for s in range(2):
            sib_cp(row, s).wait_send()
    for k in range(1, N_DP):
        gm_cp(k).wait_send()
        sc_cp(k).wait_send()
        s1_cp(k).wait_send()
    for k in range(1, n_mp):
        s2_cp(k).wait_send()


def store(u, a, b, r, u_out, a_out, b_out, r_out, sems):
    copies = [
        pltpu.make_async_copy(r, r_out.at[0, 0], sems.at[0]),
        pltpu.make_async_copy(u, u_out, sems.at[1]),
        pltpu.make_async_copy(a, a_out, sems.at[2]),
        pltpu.make_async_copy(b, b_out, sems.at[3]),
    ]
    for cp in copies:
        cp.start()
    for cp in copies:
        cp.wait()


def per_device(grads, owners, roots_prev, moment_first, moment_second):
    n_mp = lax.axis_size("mp")
    hbm = pl.BlockSpec(memory_space=pltpu.HBM)
    any_spec = pl.BlockSpec(memory_space=pl.ANY)
    vmem = pl.BlockSpec(memory_space=pltpu.VMEM)
    small = jax.ShapeDtypeStruct((4, ROWS, BS), F32)

    def body(*refs):
        kernel(n_mp, *refs)

    update, m1n, m2n, roots_new = pl.pallas_call(
        body,
        out_shape=(small, small, small, jax.ShapeDtypeStruct((2, BS, BS), BF16)),
        in_specs=[pl.BlockSpec(memory_space=pltpu.SMEM), hbm, hbm, hbm, hbm],
        out_specs=(vmem, vmem, vmem, vmem),
        scratch_shapes=[
            pltpu.VMEM((4, BS, BS), BF16),
            pltpu.VMEM((2, BS, BS), BF16),
            pltpu.VMEM((BS, BS), BF16),
            pltpu.VMEM((4, BS, BS), BF16),
            pltpu.VMEM((2, BS, BS), BF16),
            pltpu.VMEM((2, 2, PIECE, T), BF16),
            pltpu.VMEM((2, 3, PIECE, T), BF16),
            pltpu.VMEM((PIECE, T), BF16),
            pltpu.VMEM((PIECE, T), BF16),
            pltpu.VMEM((2, 2, 8, T), F32),
            pltpu.VMEM((8, 8, T), F32),
            pltpu.VMEM((3, BS, T), F32),
            pltpu.VMEM((3, BS, T), F32),
            pltpu.VMEM((BS, T), F32),
            pltpu.VMEM((BS, T), BF16),
            pltpu.VMEM((4, ROWS, BS), F32),
            pltpu.VMEM((4, ROWS, BS), BF16),
            pltpu.VMEM((8, PIECE + DIAG, T), BF16),
            pltpu.VMEM((BS, BS), F32),
            pltpu.VMEM((BS, BS), BF16),
            pltpu.VMEM((BS, BS), F32),
            pltpu.VMEM((BS, BS), BF16),
            pltpu.VMEM((BS, BS), F32),
            pltpu.VMEM((BS, BS), BF16),
            pltpu.VMEM((4, ROWS, BS), F32),
            pltpu.VMEM((8, T), F32),
            pltpu.VMEM((N_DP, 8, T), F32),
            pltpu.VMEM((8, T), F32),
            pltpu.VMEM((max(n_mp, 2), 8, T), F32),
            pltpu.VMEM((4, ROWS, BS), F32),
            pltpu.VMEM((4, ROWS, BS), F32),
            pltpu.SemaphoreType.DMA((N_SEM,)),
            pltpu.SemaphoreType.DMA((N_SEM,)),
            pltpu.SemaphoreType.DMA((LOC,)),
        ],
        compiler_params=pltpu.CompilerParams(
            collective_id=0, has_side_effects=True, vmem_limit_bytes=62 * 2**20
        ),
        name="shampoo",
    )(owners, grads, roots_prev, moment_first, moment_second)
    return pl.pallas_call(
        store,
        out_shape=(small, small, small, jax.ShapeDtypeStruct((1, 1, 2, BS, BS), BF16)),
        in_specs=[vmem] * 4,
        out_specs=[hbm] * 4,
        scratch_shapes=[pltpu.SemaphoreType.DMA((4,))],
        name="store",
    )(update, m1n, m2n, roots_new)


def solution(mesh):
    return jax.shard_map(
        per_device,
        mesh=mesh,
        in_specs=(
            P("dp", "mp", None, None),
            P("mp", None),
            P("mp", None, None, None),
            P("mp", "dp", None),
            P("mp", "dp", None),
        ),
        out_specs=(
            P("mp", "dp", None),
            P("mp", "dp", None),
            P("mp", "dp", None),
            P("dp", "mp", None, None, None),
        ),
        check_vma=False,
    )
```

```python
import jax
import jax.numpy as jnp
from jax import lax
from jax.experimental import pallas as pl
from jax.experimental.pallas import tpu as pltpu
from jax.sharding import PartitionSpec as P

MESH = pl.DeviceIdType.MESH
F32 = jnp.float32
BF16 = jnp.bfloat16
BS = 512
T = 128
N_DP = 16
ROWS = BS // N_DP
PIECE = 8 * T
DIAG = 16
OFF_TILES = ((0, 1), (0, 2), (0, 3), (1, 2), (1, 3), (2, 3))
ORDER = (2, 1, 3, 0)

CORE = 0
RAW = 2
STAT = 10
DG = 17
GRD = 25
GMX = 28
SCX = 44
AGR = 60
SIB = 64
SC1 = 68
SC2 = 84
AGS = 100
YS = 108
N_SEM = 116
LOC = 9


def dot(a, b):
    return jnp.dot(a, b, preferred_element_type=F32)


def tile_of(t):
    return pl.ds(t * T, T)


def kernel(
    n_mp,
    owners,
    grads,
    roots,
    m1_hbm,
    m2_hbm,
    update,
    m1n,
    m2n,
    roots_new,
    g_mine,
    g_other,
    left_v,
    right_v,
    tr,
    packed,
    got,
    y_out,
    y_in,
    dg_out,
    dg_in,
    g_send,
    g_recv,
    gm_loc,
    sc_loc,
    gm_rows,
    sc_rows,
    pieces,
    mat,
    mat_b,
    yy,
    yy_b,
    ee,
    ee_b,
    precond,
    s1_out,
    s1_in,
    s2_out,
    s2_in,
    m1,
    m2,
    ss,
    rs,
    ls,
):
    me = lax.axis_index("dp")
    col = lax.axis_index("mp")
    x, y, c = me // 4, (me // 2) % 2, me % 2
    even = (x % 2) == c
    keep = x // 2
    blk = 2 * c + y

    def dev(xx, yv, cc):
        return (xx * 4 + yv * 2 + cc, col)

    def xo(k):
        return lax.rem(x + k, 4)

    def rc(src, dst, i_send, i_recv, where):
        return pltpu.make_async_remote_copy(
            src_ref=src,
            dst_ref=dst,
            send_sem=ss.at[i_send],
            recv_sem=rs.at[i_recv],
            device_id=where,
            device_id_type=MESH,
        )

    barrier = pltpu.get_barrier_semaphore()
    for k in range(1, N_DP):
        pl.semaphore_signal(
            barrier, inc=1, device_id=(lax.rem(me + k, N_DP), col), device_id_type=MESH
        )
    for k in range(1, n_mp):
        pl.semaphore_signal(
            barrier, inc=1, device_id=(me, lax.rem(col + k, n_mp)), device_id_type=MESH
        )

    loads = [
        pltpu.make_async_copy(grads.at[0, 2 * c + 1 - y], g_other.at[0], ls.at[0]),
        pltpu.make_async_copy(grads.at[0, 2 * c + y], g_mine.at[0], ls.at[1]),
        pltpu.make_async_copy(roots.at[blk, 0], left_v, ls.at[2]),
    ] + [
        pltpu.make_async_copy(roots.at[b, 1], right_v.at[b], ls.at[3 + b]) for b in range(4)
    ] + [
        pltpu.make_async_copy(m1_hbm, m1, ls.at[7]),
        pltpu.make_async_copy(m2_hbm, m2, ls.at[8]),
    ]
    for cp in loads:
        cp.start()
    pl.semaphore_wait(barrier, N_DP - 1 + n_mp - 1)

    sib = dev(x, y, 1 - c)
    sends = []
    core_cp = [
        rc(grads.at[0, 2 * (1 - c) + 1 - y], g_other.at[1], CORE, CORE, sib),
        rc(grads.at[0, 2 * (1 - c) + y], g_mine.at[1], CORE + 1, CORE + 1, sib),
    ]
    for cp in core_cp:
        cp.start()
    raw_cp = []
    for n, k in enumerate(ORDER):
        cols = pl.ds(pl.multiple_of(xo(k) * T, T), T)
        for h in range(2):
            cc = c if h == 0 else 1 - c
            cp = rc(
                grads.at[0, 2 * cc + 1 - y, :, cols],
                g_mine.at[2 + h, :, cols],
                RAW + 2 * n + h,
                RAW + 2 * n + h,
                dev(x, 1 - y, cc),
            )
            cp.start()
            raw_cp.append(cp)
    sends += core_cp + raw_cp

    rows_i = lax.broadcasted_iota(jnp.int32, (T, T), 0)
    cols_i = lax.broadcasted_iota(jnp.int32, (T, T), 1)
    above = rows_i < cols_i
    below = rows_i > cols_i
    on = rows_i == cols_i

    def diag_of(t):
        return jnp.sum(jnp.where(on, t, 0.0), axis=0, keepdims=True)

    def stats(which, g):
        def pack(s, top, bot):
            for n, (i, j) in enumerate(OFF_TILES):
                if i < 2:
                    t = top[i * T : (i + 1) * T, j * T : (j + 1) * T]
                else:
                    t = bot[(i - 2) * T : (i - 1) * T, (j - 2) * T : (j - 1) * T]
                packed[which, s, tile_of(n), :] = t.astype(BF16)
            d = [
                top[0:T, 0:T],
                top[T : 2 * T, T : 2 * T],
                bot[0:T, 0:T],
                bot[T : 2 * T, T : 2 * T],
            ]
            packed[which, s, tile_of(6), :] = jnp.where(above, d[0], d[1]).astype(BF16)
            packed[which, s, tile_of(7), :] = jnp.where(above, d[2], d[3]).astype(BF16)
            dg_out[which, s] = jnp.zeros((8, T), F32)
            for n in range(4):
                dg_out[which, s, n : n + 1, :] = diag_of(d[n])

        for h in range(2):
            tr[h] = g[h].T
        h2 = BS // 2
        top = dot(g[0, :h2, :], tr[0]) + dot(g[1, :h2, :], tr[1])
        bot = dot(g[0, h2:, :], tr[0, :, h2:]) + dot(g[1, h2:, :], tr[1, :, h2:])
        pack(0, top, bot)
        top = dot(tr[0, :h2, :], g[0]) + dot(tr[1, :h2, :], g[1])
        bot = dot(tr[0, h2:, :], g[0, :, h2:]) + dot(tr[1, h2:, :], g[1, :, h2:])
        pack(1, top, bot)

    def stat_cp(which, s):
        xt = 2 * s + c
        k = lax.rem(xt - x + 4, 4)
        slot = jnp.maximum(k - 1, 0)
        return k, rc(
            packed.at[which, s],
            got.at[which, slot],
            STAT + 2 * which + s,
            STAT + 3 * which + slot,
            dev(xt, y, c),
        )

    def dg_cp(which, s):
        yt = 1 - y if which == 0 else y
        return rc(
            dg_out.at[which, s],
            dg_in.at[2 * x + y],
            DG + 2 * which + s,
            DG + 2 * x + y,
            dev(2 * s + c, yt, c),
        )

    def stat_sends(which, act):
        for s in range(2):
            k, cp = stat_cp(which, s)
            pl.when(k != 0)(lambda cp=cp: act(cp))
            cp2 = dg_cp(which, s)
            if which == 0:
                act(cp2)
            else:
                pl.when(k != 0)(lambda cp2=cp2: act(cp2))

    loads[0].wait()
    core_cp[0].wait_recv()
    stats(0, g_other)
    stat_sends(0, lambda cp: cp.start())
    loads[1].wait()
    core_cp[1].wait_recv()
    stats(1, g_mine)
    stat_sends(1, lambda cp: cp.start())

    def raw_sum(n):
        cols = pl.ds(pl.multiple_of(xo(ORDER[n]) * T, T), T)
        raw_cp[2 * n].wait_recv()
        raw_cp[2 * n + 1].wait_recv()
        t = g_mine[0, :, cols].astype(F32) + g_mine[1, :, cols].astype(F32)
        return t + (g_mine[2, :, cols].astype(F32) + g_mine[3, :, cols].astype(F32))

    grd_cp = []

    def grad_chunk(n):
        k = ORDER[n]
        g_send[k - 1] = raw_sum(n)
        cp = rc(g_send.at[k - 1], g_recv.at[k - 1], GRD + k - 1, GRD + k - 1, dev(xo(k), y, c))
        cp.start()
        grd_cp.append(cp)

    def wait_stats(which):
        for slot in range(3):
            rc(
                packed.at[which, 0],
                got.at[which, slot],
                STAT,
                STAT + 3 * which + slot,
                dev(x, 1 - y, c),
            ).wait_recv()

    def stat_tile(which, n):
        t = packed[which, keep, tile_of(n), :].astype(F32)
        for slot in range(3):
            t = t + got[which, slot, tile_of(n), :].astype(F32)
        return t

    y_cp = [
        rc(y_out.at[tile_of(n)], y_in.at[tile_of(n)], YS + n, YS + n, dev(x, 1 - y, c))
        for n in range(8)
    ]

    grad_chunk(0)

    @pl.when(even)
    def _():
        wait_stats(0)
        for n in range(8):
            y_out[tile_of(n), :] = stat_tile(0, n).astype(BF16)
            y_cp[n].start()

    grad_chunk(1)

    my_piece = 4 * c + 2 * y + keep

    def ring_cp(row, k):
        yr = y if row == 0 else 1 - y
        ref = pieces.at[4 * c + 2 * yr + keep]
        return rc(ref, ref, AGS + 4 * row + k - 1, AGR + 2 * row + keep, dev(xo(k), y, c))

    def ycopy():
        ref = pieces.at[my_piece]
        return rc(ref, ref, AGS + 3, AGR + 2 + keep, dev(x, 1 - y, c))

    grad_chunk(2)

    def piece_at(row, s):
        yr = y if row == 0 else 1 - y
        return pieces.at[4 * c + 2 * yr + s]

    def other_piece_at(row, s):
        yr = y if row == 0 else 1 - y
        return pieces.at[4 * (1 - c) + 2 * yr + s]

    def sib_cp(row, s):
        return rc(piece_at(row, s), piece_at(row, s), SIB + 2 * row + s, SIB + 2 * row + s, sib)

    def over_cp(s):
        ref = piece_at(0, s)
        return rc(ref, ref, AGS + s, AGR + 2 + s, dev(x, 1 - y, c))

    def ag_wait(row, s):
        ref = piece_at(row, s)
        rc(ref, ref, AGR, AGR + 2 * row + s, dev(x, 1 - y, c)).wait_recv()

    own = raw_sum(3)
    for k in (2, 1, 3):
        grd_cp[(2, 1, 3).index(k)].wait_recv()
        own = own + g_recv[k - 1]
    gm_loc[...] = own * (1.0 / N_DP)
    my_cols = pl.ds(pl.multiple_of(x * T, T), T)

    def gm_cp(k):
        to = lax.rem(me + k, N_DP)
        r = pl.ds(pl.multiple_of(to * ROWS, ROWS), ROWS)
        return rc(gm_loc.at[r], gm_rows.at[blk, :, my_cols], GMX + k, GMX + k, (to, col))

    def sc_cp(k):
        to = lax.rem(me + k, N_DP)
        r = pl.ds(pl.multiple_of(to * ROWS, ROWS), ROWS)
        return rc(sc_loc.at[r], sc_rows.at[blk, :, my_cols], SCX + k, SCX + k, (to, col))

    my_rows = pl.ds(pl.multiple_of(me * ROWS, ROWS), ROWS)
    for k in range(1, N_DP):
        gm_cp(k).start()
    loads[2].wait()
    sc_loc[...] = dot(left_v[...], gm_loc[...].astype(BF16)).astype(BF16)
    for k in range(1, N_DP):
        sc_cp(k).start()
    gm_rows[blk, :, my_cols] = gm_loc[my_rows, :]
    sc_rows[blk, :, my_cols] = sc_loc[my_rows, :]

    @pl.when(even)
    def _():
        for cp in y_cp:
            cp.wait_recv()
        wait_stats(1)
        dsum = dg_out[1, keep]
        for sender in range(8):

            @pl.when(sender != 2 * x + y)
            def _():
                rc(
                    dg_out.at[0, 0], dg_in.at[sender], DG, DG + sender, dev(x, 1 - y, c)
                ).wait_recv()

        for sender in range(8):
            dsum = dsum + jnp.where(sender != 2 * x + y, dg_in[sender], 0.0)
        dsum = dsum * (1.0 / N_DP) + 0.0001

        def full_tile(n):
            return (stat_tile(1, n) + y_in[tile_of(n), :].astype(F32)) * (1.0 / N_DP)

        off_sq = jnp.zeros((T, T), F32)
        for n, (i, j) in enumerate(OFF_TILES):
            t = full_tile(n)
            off_sq = off_sq + t * t
            mat[tile_of(i), tile_of(j)] = t
            mat[tile_of(j), tile_of(i)] = t.T
        for n, (i, j) in ((6, (0, 1)), (7, (2, 3))):
            t = full_tile(n)
            tt = t.T
            d0, d1 = dsum[i : i + 1, :], dsum[j : j + 1, :]
            off_sq = off_sq + jnp.where(on, 0.0, t * t)
            mat[tile_of(i), tile_of(i)] = jnp.where(above, t, jnp.where(below, tt, d0))
            mat[tile_of(j), tile_of(j)] = jnp.where(below, t, jnp.where(above, tt, d1))
        total = 2.0 * jnp.sum(off_sq) + jnp.sum(
            jnp.where(lax.broadcasted_iota(jnp.int32, (8, T), 0) < 4, dsum * dsum, 0.0)
        )
        inv = 1.0 / jnp.sqrt(jnp.full((1, 1), total, F32))
        mat[...] = mat[...] * inv
        mat_b[...] = mat[...].astype(BF16)
        yy[...] = mat[...] * -0.25
        yy_b[...] = yy[...].astype(BF16)
        scale = 1.25
        for _step in range(2):
            ee[...] = (dot(mat_b[...], mat_b[...]) - 10.0 * mat[...]) * (1.0 / 16.0)
            ee_b[...] = ee[...].astype(BF16)
            ee_b[...] = (3.125 * ee[...] + dot(ee_b[...], ee_b[...])).astype(BF16)
            mat[...] = (625.0 / 256.0) * mat[...] + dot(mat_b[...], ee_b[...])
            mat_b[...] = mat[...].astype(BF16)
            yy[...] = (
                1.25 * yy[...] - (scale / 4.0) * mat[...] - 0.25 * dot(yy_b[...], mat_b[...])
            )
            yy_b[...] = yy[...].astype(BF16)
            scale = scale * 1.25
        for n, (i, j) in enumerate(OFF_TILES):
            pieces[my_piece, tile_of(n), :] = yy[tile_of(i), tile_of(j)].astype(BF16)
        for n, (i, j) in ((6, (0, 1)), (7, (2, 3))):
            pieces[my_piece, tile_of(n), :] = jnp.where(
                above, yy[tile_of(i), tile_of(i)], yy[tile_of(j), tile_of(j)]
            ).astype(BF16)
        ds = [diag_of(yy[tile_of(i), tile_of(i)]) + scale for i in range(4)]
        pieces[my_piece, PIECE : PIECE + DIAG, :] = jnp.concatenate(
            ds + [jnp.zeros((DIAG - 4, T), F32)], axis=0
        ).astype(BF16)
        ycopy().start()
        for k in (1, 3, 2):
            ring_cp(0, k).start()

    for k in range(1, N_DP):
        gm_cp(k).wait_recv()
    loads[7].wait()
    loads[8].wait()
    g = gm_rows[...]
    first = 0.9 * m1[...] + 0.1 * g
    second = 0.95 * m2[...] + 0.05 * g * g
    m1n[...] = first
    m2n[...] = second
    adam = first / (jnp.sqrt(second) + 1e-08)
    adam_sq = jnp.sum(adam * adam)
    for b in range(4):
        loads[3 + b].wait()
    for k in range(1, N_DP):
        sc_cp(k).wait_recv()
    pre_sq = jnp.zeros((ROWS, BS), F32)
    for b in range(4):
        p = dot(sc_rows[b], right_v[b])
        precond[b] = p
        pre_sq = pre_sq + p * p
    pre_sq = jnp.sum(pre_sq)
    mine = jnp.where(lax.broadcasted_iota(jnp.int32, (1, T), 1) < T // 2, adam_sq, pre_sq)
    s1_out[...] = mine

    def s1_cp(k):
        return rc(s1_out, s1_in.at[k], SC1 + k, SC1 + k, (lax.rem(me + k, N_DP), col))

    def s2_cp(k):
        return rc(s2_out, s2_in.at[k], SC2 + k, SC2 + k, (me, lax.rem(col + k, n_mp)))

    for k in range(1, N_DP):
        s1_cp(k).start()

    @pl.when(even)
    def _():
        sib_cp(0, keep).start()
        ag_wait(1, keep)
        ring_cp(1, 2).start()
        sib_cp(1, keep).start()

    @pl.when(jnp.logical_not(even))
    def _():
        for s in range(2):
            ag_wait(0, s)
            over_cp(s).start()
            sib_cp(0, s).start()

    for k in range(1, N_DP):
        s1_cp(k).wait_recv()
    for k in range(1, N_DP):
        mine = mine + s1_in[k]
    s2_out[...] = mine
    for k in range(1, n_mp):
        s2_cp(k).start()

    @pl.when(even)
    def _():
        for row in range(2):
            ag_wait(row, 1 - keep)
            sib_cp(row, 1 - keep).start()

    @pl.when(jnp.logical_not(even))
    def _():
        for s in range(2):
            ag_wait(1, s)
            sib_cp(1, s).start()

    for row in range(2):
        for s in range(2):
            ref = other_piece_at(row, s)
            rc(ref, ref, SIB, SIB + 2 * row + s, sib).wait_recv()

    first_id, second_id, n_mine = jnp.int32(0), jnp.int32(0), jnp.int32(0)
    for i in range(8):
        hit = owners[0, i] == me
        first_id = jnp.where(hit & (n_mine == 0), i, first_id)
        second_id = jnp.where(hit & (n_mine == 1), i, second_id)
        n_mine = n_mine + jnp.where(hit, 1, 0)
    for slot, idx in ((0, first_id), (1, second_id)):
        filled = n_mine > slot

        def piece_tile(n):
            return jnp.where(filled, pieces[idx, tile_of(n), :].astype(F32), 0.0)

        for n, (i, j) in enumerate(OFF_TILES):
            t = piece_tile(n)
            roots_new[slot, tile_of(i), tile_of(j)] = t.astype(BF16)
            roots_new[slot, tile_of(j), tile_of(i)] = t.T.astype(BF16)
        dg = jnp.where(filled, pieces[idx, PIECE : PIECE + DIAG, :].astype(F32), 0.0)
        for n, (i, j) in ((6, (0, 1)), (7, (2, 3))):
            t = piece_tile(n)
            tt = t.T
            d0, d1 = dg[i : i + 1, :], dg[j : j + 1, :]
            roots_new[slot, tile_of(i), tile_of(i)] = jnp.where(
                above, t, jnp.where(below, tt, d0)
            ).astype(BF16)
            roots_new[slot, tile_of(j), tile_of(j)] = jnp.where(
                below, t, jnp.where(above, tt, d1)
            ).astype(BF16)

    for k in range(1, n_mp):
        s2_cp(k).wait_recv()
    for k in range(1, n_mp):
        mine = mine + s2_in[k]
    ratio = jnp.sqrt(mine[:, :1]) / jnp.sqrt(mine[:, T - 1 :] + 1e-06)
    for b in range(4):
        update[b] = precond[b] * ratio

    for cp in sends + grd_cp:
        cp.wait_send()
    stat_sends(0, lambda cp: cp.wait_send())
    stat_sends(1, lambda cp: cp.wait_send())

    @pl.when(even)
    def _():
        for cp in y_cp:
            cp.wait_send()
        ycopy().wait_send()
        for k in (1, 3, 2):
            ring_cp(0, k).wait_send()
        ring_cp(1, 2).wait_send()

    @pl.when(jnp.logical_not(even))
    def _():
        for s in range(2):
            over_cp(s).wait_send()

    for row in range(2):
        for s in range(2):
            sib_cp(row, s).wait_send()
    for k in range(1, N_DP):
        gm_cp(k).wait_send()
        sc_cp(k).wait_send()
        s1_cp(k).wait_send()
    for k in range(1, n_mp):
        s2_cp(k).wait_send()


def store(u, a, b, r, u_out, a_out, b_out, r_out, sems):
    copies = [
        pltpu.make_async_copy(r, r_out.at[0, 0], sems.at[0]),
        pltpu.make_async_copy(u, u_out, sems.at[1]),
        pltpu.make_async_copy(a, a_out, sems.at[2]),
        pltpu.make_async_copy(b, b_out, sems.at[3]),
    ]
    for cp in copies:
        cp.start()
    for cp in copies:
        cp.wait()


def per_device(grads, owners, roots_prev, moment_first, moment_second):
    n_mp = lax.axis_size("mp")
    hbm = pl.BlockSpec(memory_space=pltpu.HBM)
    any_spec = pl.BlockSpec(memory_space=pl.ANY)
    vmem = pl.BlockSpec(memory_space=pltpu.VMEM)
    small = jax.ShapeDtypeStruct((4, ROWS, BS), F32)

    def body(*refs):
        kernel(n_mp, *refs)

    update, m1n, m2n, roots_new = pl.pallas_call(
        body,
        out_shape=(small, small, small, jax.ShapeDtypeStruct((2, BS, BS), BF16)),
        in_specs=[pl.BlockSpec(memory_space=pltpu.SMEM), hbm, hbm, hbm, hbm],
        out_specs=(vmem, vmem, vmem, vmem),
        scratch_shapes=[
            pltpu.VMEM((4, BS, BS), BF16),
            pltpu.VMEM((2, BS, BS), BF16),
            pltpu.VMEM((BS, BS), BF16),
            pltpu.VMEM((4, BS, BS), BF16),
            pltpu.VMEM((2, BS, BS), BF16),
            pltpu.VMEM((2, 2, PIECE, T), BF16),
            pltpu.VMEM((2, 3, PIECE, T), BF16),
            pltpu.VMEM((PIECE, T), BF16),
            pltpu.VMEM((PIECE, T), BF16),
            pltpu.VMEM((2, 2, 8, T), F32),
            pltpu.VMEM((8, 8, T), F32),
            pltpu.VMEM((3, BS, T), F32),
            pltpu.VMEM((3, BS, T), F32),
            pltpu.VMEM((BS, T), F32),
            pltpu.VMEM((BS, T), BF16),
            pltpu.VMEM((4, ROWS, BS), F32),
            pltpu.VMEM((4, ROWS, BS), BF16),
            pltpu.VMEM((8, PIECE + DIAG, T), BF16),
            pltpu.VMEM((BS, BS), F32),
            pltpu.VMEM((BS, BS), BF16),
            pltpu.VMEM((BS, BS), F32),
            pltpu.VMEM((BS, BS), BF16),
            pltpu.VMEM((BS, BS), F32),
            pltpu.VMEM((BS, BS), BF16),
            pltpu.VMEM((4, ROWS, BS), F32),
            pltpu.VMEM((1, T), F32),
            pltpu.VMEM((N_DP, 1, T), F32),
            pltpu.VMEM((1, T), F32),
            pltpu.VMEM((max(n_mp, 2), 1, T), F32),
            pltpu.VMEM((4, ROWS, BS), F32),
            pltpu.VMEM((4, ROWS, BS), F32),
            pltpu.SemaphoreType.DMA((N_SEM,)),
            pltpu.SemaphoreType.DMA((N_SEM,)),
            pltpu.SemaphoreType.DMA((LOC,)),
        ],
        compiler_params=pltpu.CompilerParams(
            collective_id=0, has_side_effects=True, vmem_limit_bytes=62 * 2**20
        ),
        name="shampoo",
    )(owners.T, grads, roots_prev, moment_first, moment_second)
    return pl.pallas_call(
        store,
        out_shape=(small, small, small, jax.ShapeDtypeStruct((1, 1, 2, BS, BS), BF16)),
        in_specs=[vmem] * 4,
        out_specs=[hbm] * 4,
        scratch_shapes=[pltpu.SemaphoreType.DMA((4,))],
        name="store",
    )(update, m1n, m2n, roots_new)


def solution(mesh):
    return jax.shard_map(
        per_device,
        mesh=mesh,
        in_specs=(
            P("dp", "mp", None, None),
            P("mp", None),
            P("mp", None, None, None),
            P("mp", "dp", None),
            P("mp", "dp", None),
        ),
        out_specs=(
            P("mp", "dp", None),
            P("mp", "dp", None),
            P("mp", "dp", None),
            P("dp", "mp", None, None, None),
        ),
        check_vma=False,
    )
```

```python
import jax
import jax.numpy as jnp
from jax import lax
from jax.experimental import pallas as pl
from jax.experimental.pallas import tpu as pltpu
from jax.sharding import PartitionSpec as P

MESH = pl.DeviceIdType.MESH
F32 = jnp.float32
BF16 = jnp.bfloat16
BS = 512
T = 128
N_DP = 16
ROWS = BS // N_DP
PIECE = 8 * T
DIAG = 16
OFF_TILES = ((0, 1), (0, 2), (0, 3), (1, 2), (1, 3), (2, 3))
ORDER = (2, 1, 3, 0)

CORE = 0
RAW = 2
STAT = 10
DG = 17
GRD = 25
GMX = 28
SCX = 44
AGR = 60
SIB = 64
SC1 = 68
SC2 = 84
AGS = 100
YS = 108
N_SEM = 116
LOC = 9


def dot(a, b):
    return jnp.dot(a, b, preferred_element_type=F32)


def tile_of(t):
    return pl.ds(t * T, T)


def kernel(
    n_mp,
    owners,
    grads,
    roots,
    m1_hbm,
    m2_hbm,
    update,
    m1n,
    m2n,
    roots_new,
    g_mine,
    g_other,
    left_v,
    right_v,
    tr,
    packed,
    got,
    y_out,
    y_in,
    dg_out,
    dg_in,
    g_send,
    g_recv,
    gm_loc,
    sc_loc,
    gm_rows,
    sc_rows,
    pieces,
    mat,
    mat_b,
    yy,
    yy_b,
    ee,
    ee_b,
    precond,
    s1_out,
    s1_in,
    s2_out,
    s2_in,
    m1,
    m2,
    ss,
    rs,
    ls,
):
    me = lax.axis_index("dp")
    col = lax.axis_index("mp")
    x, y, c = me // 4, (me // 2) % 2, me % 2
    even = (x % 2) == c
    keep = x // 2
    blk = 2 * c + y

    def dev(xx, yv, cc):
        return (xx * 4 + yv * 2 + cc, col)

    def xo(k):
        return lax.rem(x + k, 4)

    def rc(src, dst, i_send, i_recv, where):
        return pltpu.make_async_remote_copy(
            src_ref=src,
            dst_ref=dst,
            send_sem=ss.at[i_send],
            recv_sem=rs.at[i_recv],
            device_id=where,
            device_id_type=MESH,
        )

    barrier = pltpu.get_barrier_semaphore()
    for k in range(1, N_DP):
        pl.semaphore_signal(
            barrier, inc=1, device_id=(lax.rem(me + k, N_DP), col), device_id_type=MESH
        )
    for k in range(1, n_mp):
        pl.semaphore_signal(
            barrier, inc=1, device_id=(me, lax.rem(col + k, n_mp)), device_id_type=MESH
        )

    loads = [
        pltpu.make_async_copy(grads.at[0, 2 * c + 1 - y], g_other.at[0], ls.at[0]),
        pltpu.make_async_copy(grads.at[0, 2 * c + y], g_mine.at[0], ls.at[1]),
        pltpu.make_async_copy(roots.at[blk, 0], left_v, ls.at[2]),
    ] + [
        pltpu.make_async_copy(roots.at[b, 1], right_v.at[b], ls.at[3 + b]) for b in range(4)
    ] + [
        pltpu.make_async_copy(m1_hbm, m1, ls.at[7]),
        pltpu.make_async_copy(m2_hbm, m2, ls.at[8]),
    ]
    for cp in loads:
        cp.start()
    pl.semaphore_wait(barrier, N_DP - 1 + n_mp - 1)

    sib = dev(x, y, 1 - c)
    sends = []
    core_cp = [
        rc(grads.at[0, 2 * (1 - c) + 1 - y], g_other.at[1], CORE, CORE, sib),
        rc(grads.at[0, 2 * (1 - c) + y], g_mine.at[1], CORE + 1, CORE + 1, sib),
    ]
    for cp in core_cp:
        cp.start()
    raw_cp = []
    for n, k in enumerate(ORDER):
        cols = pl.ds(pl.multiple_of(xo(k) * T, T), T)
        for h in range(2):
            cc = c if h == 0 else 1 - c
            cp = rc(
                grads.at[0, 2 * cc + 1 - y, :, cols],
                g_mine.at[2 + h, :, cols],
                RAW + 2 * n + h,
                RAW + 2 * n + h,
                dev(x, 1 - y, cc),
            )
            if n < 2:
                cp.start()
            raw_cp.append(cp)
    sends += core_cp + raw_cp

    rows_i = lax.broadcasted_iota(jnp.int32, (T, T), 0)
    cols_i = lax.broadcasted_iota(jnp.int32, (T, T), 1)
    above = rows_i < cols_i
    below = rows_i > cols_i
    on = rows_i == cols_i

    def diag_of(t):
        return jnp.sum(jnp.where(on, t, 0.0), axis=0, keepdims=True)

    def stats(which, g):
        def pack(s, top, bot):
            for n, (i, j) in enumerate(OFF_TILES):
                if i < 2:
                    t = top[i * T : (i + 1) * T, j * T : (j + 1) * T]
                else:
                    t = bot[(i - 2) * T : (i - 1) * T, (j - 2) * T : (j - 1) * T]
                packed[which, s, tile_of(n), :] = t.astype(BF16)
            d = [
                top[0:T, 0:T],
                top[T : 2 * T, T : 2 * T],
                bot[0:T, 0:T],
                bot[T : 2 * T, T : 2 * T],
            ]
            packed[which, s, tile_of(6), :] = jnp.where(above, d[0], d[1]).astype(BF16)
            packed[which, s, tile_of(7), :] = jnp.where(above, d[2], d[3]).astype(BF16)
            dg_out[which, s] = jnp.zeros((8, T), F32)
            for n in range(4):
                dg_out[which, s, n : n + 1, :] = diag_of(d[n])

        for h in range(2):
            tr[h] = g[h].T
        h2 = BS // 2
        top = dot(g[0, :h2, :], tr[0]) + dot(g[1, :h2, :], tr[1])
        bot = dot(g[0, h2:, :], tr[0, :, h2:]) + dot(g[1, h2:, :], tr[1, :, h2:])
        pack(0, top, bot)
        top = dot(tr[0, :h2, :], g[0]) + dot(tr[1, :h2, :], g[1])
        bot = dot(tr[0, h2:, :], g[0, :, h2:]) + dot(tr[1, h2:, :], g[1, :, h2:])
        pack(1, top, bot)

    def stat_cp(which, s):
        xt = 2 * s + c
        k = lax.rem(xt - x + 4, 4)
        slot = jnp.maximum(k - 1, 0)
        return k, rc(
            packed.at[which, s],
            got.at[which, slot],
            STAT + 2 * which + s,
            STAT + 3 * which + slot,
            dev(xt, y, c),
        )

    def dg_cp(which, s):
        yt = 1 - y if which == 0 else y
        return rc(
            dg_out.at[which, s],
            dg_in.at[2 * x + y],
            DG + 2 * which + s,
            DG + 2 * x + y,
            dev(2 * s + c, yt, c),
        )

    def stat_sends(which, act):
        for s in range(2):
            k, cp = stat_cp(which, s)
            pl.when(k != 0)(lambda cp=cp: act(cp))
            cp2 = dg_cp(which, s)
            if which == 0:
                act(cp2)
            else:
                pl.when(k != 0)(lambda cp2=cp2: act(cp2))

    loads[0].wait()
    core_cp[0].wait_recv()
    stats(0, g_other)
    stat_sends(0, lambda cp: cp.start())
    loads[1].wait()
    core_cp[1].wait_recv()
    stats(1, g_mine)
    stat_sends(1, lambda cp: cp.start())

    def raw_sum(n):
        cols = pl.ds(pl.multiple_of(xo(ORDER[n]) * T, T), T)
        raw_cp[2 * n].wait_recv()
        raw_cp[2 * n + 1].wait_recv()
        t = g_mine[0, :, cols].astype(F32) + g_mine[1, :, cols].astype(F32)
        return t + (g_mine[2, :, cols].astype(F32) + g_mine[3, :, cols].astype(F32))

    grd_cp = []

    def grad_chunk(n):
        k = ORDER[n]
        g_send[k - 1] = raw_sum(n)
        for cp in raw_cp[2 * (n + 2) : 2 * (n + 2) + 2]:
            cp.start()
        cp = rc(g_send.at[k - 1], g_recv.at[k - 1], GRD + k - 1, GRD + k - 1, dev(xo(k), y, c))
        cp.start()
        grd_cp.append(cp)

    def wait_stats(which):
        for slot in range(3):
            rc(
                packed.at[which, 0],
                got.at[which, slot],
                STAT,
                STAT + 3 * which + slot,
                dev(x, 1 - y, c),
            ).wait_recv()

    def stat_tile(which, n):
        t = packed[which, keep, tile_of(n), :].astype(F32)
        for slot in range(3):
            t = t + got[which, slot, tile_of(n), :].astype(F32)
        return t

    y_cp = [
        rc(y_out.at[tile_of(n)], y_in.at[tile_of(n)], YS + n, YS + n, dev(x, 1 - y, c))
        for n in range(8)
    ]

    grad_chunk(0)

    @pl.when(even)
    def _():
        wait_stats(0)
        for n in range(8):
            y_out[tile_of(n), :] = stat_tile(0, n).astype(BF16)
            y_cp[n].start()

    grad_chunk(1)

    my_piece = 4 * c + 2 * y + keep

    def ring_cp(row, k):
        yr = y if row == 0 else 1 - y
        ref = pieces.at[4 * c + 2 * yr + keep]
        return rc(ref, ref, AGS + 4 * row + k - 1, AGR + 2 * row + keep, dev(xo(k), y, c))

    def ycopy():
        ref = pieces.at[my_piece]
        return rc(ref, ref, AGS + 3, AGR + 2 + keep, dev(x, 1 - y, c))

    grad_chunk(2)

    def piece_at(row, s):
        yr = y if row == 0 else 1 - y
        return pieces.at[4 * c + 2 * yr + s]

    def other_piece_at(row, s):
        yr = y if row == 0 else 1 - y
        return pieces.at[4 * (1 - c) + 2 * yr + s]

    def sib_cp(row, s):
        return rc(piece_at(row, s), piece_at(row, s), SIB + 2 * row + s, SIB + 2 * row + s, sib)

    def over_cp(s):
        ref = piece_at(0, s)
        return rc(ref, ref, AGS + s, AGR + 2 + s, dev(x, 1 - y, c))

    def ag_wait(row, s):
        ref = piece_at(row, s)
        rc(ref, ref, AGR, AGR + 2 * row + s, dev(x, 1 - y, c)).wait_recv()

    own = raw_sum(3)
    for k in (2, 1, 3):
        grd_cp[(2, 1, 3).index(k)].wait_recv()
        own = own + g_recv[k - 1]
    gm_loc[...] = own * (1.0 / N_DP)
    my_cols = pl.ds(pl.multiple_of(x * T, T), T)

    def gm_cp(k):
        to = lax.rem(me + k, N_DP)
        r = pl.ds(pl.multiple_of(to * ROWS, ROWS), ROWS)
        return rc(gm_loc.at[r], gm_rows.at[blk, :, my_cols], GMX + k, GMX + k, (to, col))

    def sc_cp(k):
        to = lax.rem(me + k, N_DP)
        r = pl.ds(pl.multiple_of(to * ROWS, ROWS), ROWS)
        return rc(sc_loc.at[r], sc_rows.at[blk, :, my_cols], SCX + k, SCX + k, (to, col))

    my_rows = pl.ds(pl.multiple_of(me * ROWS, ROWS), ROWS)
    for k in range(1, N_DP):
        gm_cp(k).start()
    loads[2].wait()
    sc_loc[...] = dot(left_v[...], gm_loc[...].astype(BF16)).astype(BF16)
    for k in range(1, N_DP):
        sc_cp(k).start()
    gm_rows[blk, :, my_cols] = gm_loc[my_rows, :]
    sc_rows[blk, :, my_cols] = sc_loc[my_rows, :]

    @pl.when(even)
    def _():
        for cp in y_cp:
            cp.wait_recv()
        wait_stats(1)
        dsum = dg_out[1, keep]
        for sender in range(8):

            @pl.when(sender != 2 * x + y)
            def _():
                rc(
                    dg_out.at[0, 0], dg_in.at[sender], DG, DG + sender, dev(x, 1 - y, c)
                ).wait_recv()

        for sender in range(8):
            dsum = dsum + jnp.where(sender != 2 * x + y, dg_in[sender], 0.0)
        dsum = dsum * (1.0 / N_DP) + 0.0001

        def full_tile(n):
            return (stat_tile(1, n) + y_in[tile_of(n), :].astype(F32)) * (1.0 / N_DP)

        off_sq = jnp.zeros((T, T), F32)
        for n, (i, j) in enumerate(OFF_TILES):
            t = full_tile(n)
            off_sq = off_sq + t * t
            mat[tile_of(i), tile_of(j)] = t
            mat[tile_of(j), tile_of(i)] = t.T
        for n, (i, j) in ((6, (0, 1)), (7, (2, 3))):
            t = full_tile(n)
            tt = t.T
            d0, d1 = dsum[i : i + 1, :], dsum[j : j + 1, :]
            off_sq = off_sq + jnp.where(on, 0.0, t * t)
            mat[tile_of(i), tile_of(i)] = jnp.where(above, t, jnp.where(below, tt, d0))
            mat[tile_of(j), tile_of(j)] = jnp.where(below, t, jnp.where(above, tt, d1))
        total = 2.0 * jnp.sum(off_sq) + jnp.sum(
            jnp.where(lax.broadcasted_iota(jnp.int32, (8, T), 0) < 4, dsum * dsum, 0.0)
        )
        inv = 1.0 / jnp.sqrt(jnp.full((1, 1), total, F32))
        mat[...] = mat[...] * inv
        mat_b[...] = mat[...].astype(BF16)
        yy[...] = mat[...] * -0.25
        yy_b[...] = yy[...].astype(BF16)
        scale = 1.25
        for _step in range(2):
            ee[...] = (dot(mat_b[...], mat_b[...]) - 10.0 * mat[...]) * (1.0 / 16.0)
            ee_b[...] = ee[...].astype(BF16)
            ee_b[...] = (3.125 * ee[...] + dot(ee_b[...], ee_b[...])).astype(BF16)
            mat[...] = (625.0 / 256.0) * mat[...] + dot(mat_b[...], ee_b[...])
            mat_b[...] = mat[...].astype(BF16)
            yy[...] = (
                1.25 * yy[...] - (scale / 4.0) * mat[...] - 0.25 * dot(yy_b[...], mat_b[...])
            )
            yy_b[...] = yy[...].astype(BF16)
            scale = scale * 1.25
        for n, (i, j) in enumerate(OFF_TILES):
            pieces[my_piece, tile_of(n), :] = yy[tile_of(i), tile_of(j)].astype(BF16)
        for n, (i, j) in ((6, (0, 1)), (7, (2, 3))):
            pieces[my_piece, tile_of(n), :] = jnp.where(
                above, yy[tile_of(i), tile_of(i)], yy[tile_of(j), tile_of(j)]
            ).astype(BF16)
        ds = [diag_of(yy[tile_of(i), tile_of(i)]) + scale for i in range(4)]
        pieces[my_piece, PIECE : PIECE + DIAG, :] = jnp.concatenate(
            ds + [jnp.zeros((DIAG - 4, T), F32)], axis=0
        ).astype(BF16)
        ycopy().start()
        for k in (1, 3, 2):
            ring_cp(0, k).start()

    for cp in sends + grd_cp:
        cp.wait_send()
    stat_sends(0, lambda cp: cp.wait_send())
    stat_sends(1, lambda cp: cp.wait_send())

    for k in range(1, N_DP):
        gm_cp(k).wait_recv()
    loads[7].wait()
    loads[8].wait()
    g = gm_rows[...]
    first = 0.9 * m1[...] + 0.1 * g
    second = 0.95 * m2[...] + 0.05 * g * g
    m1n[...] = first
    m2n[...] = second
    adam = first / (jnp.sqrt(second) + 1e-08)
    adam_sq = jnp.sum(adam * adam)
    for b in range(4):
        loads[3 + b].wait()
    for k in range(1, N_DP):
        sc_cp(k).wait_recv()
    pre_sq = jnp.zeros((ROWS, BS), F32)
    for b in range(4):
        p = dot(sc_rows[b], right_v[b])
        precond[b] = p
        pre_sq = pre_sq + p * p
    pre_sq = jnp.sum(pre_sq)
    mine = jnp.where(lax.broadcasted_iota(jnp.int32, (1, T), 1) < T // 2, adam_sq, pre_sq)
    s1_out[...] = mine

    def s1_cp(k):
        return rc(s1_out, s1_in.at[k], SC1 + k, SC1 + k, (lax.rem(me + k, N_DP), col))

    def s2_cp(k):
        return rc(s2_out, s2_in.at[k], SC2 + k, SC2 + k, (me, lax.rem(col + k, n_mp)))

    for k in range(1, N_DP):
        s1_cp(k).start()
    for k in range(1, N_DP):
        gm_cp(k).wait_send()
        sc_cp(k).wait_send()

    @pl.when(even)
    def _():
        sib_cp(0, keep).start()
        ag_wait(1, keep)
        ring_cp(1, 2).start()
        sib_cp(1, keep).start()

    @pl.when(jnp.logical_not(even))
    def _():
        for s in range(2):
            ag_wait(0, s)
            over_cp(s).start()
            sib_cp(0, s).start()

    for k in range(1, N_DP):
        s1_cp(k).wait_recv()
    for k in range(1, N_DP):
        mine = mine + s1_in[k]
    s2_out[...] = mine
    for k in range(1, n_mp):
        s2_cp(k).start()

    @pl.when(even)
    def _():
        for row in range(2):
            ag_wait(row, 1 - keep)
            sib_cp(row, 1 - keep).start()

    @pl.when(jnp.logical_not(even))
    def _():
        for s in range(2):
            ag_wait(1, s)
            sib_cp(1, s).start()

    for row in range(2):
        for s in range(2):
            ref = other_piece_at(row, s)
            rc(ref, ref, SIB, SIB + 2 * row + s, sib).wait_recv()

    first_id, second_id, n_mine = jnp.int32(0), jnp.int32(0), jnp.int32(0)
    for i in range(8):
        hit = owners[0, i] == me
        first_id = jnp.where(hit & (n_mine == 0), i, first_id)
        second_id = jnp.where(hit & (n_mine == 1), i, second_id)
        n_mine = n_mine + jnp.where(hit, 1, 0)
    for slot, idx in ((0, first_id), (1, second_id)):
        filled = n_mine > slot

        def piece_tile(n):
            return jnp.where(filled, pieces[idx, tile_of(n), :].astype(F32), 0.0)

        for n, (i, j) in enumerate(OFF_TILES):
            t = piece_tile(n).astype(BF16)
            roots_new[slot, tile_of(i), tile_of(j)] = t
            roots_new[slot, tile_of(j), tile_of(i)] = t.T
        dg = jnp.where(filled, pieces[idx, PIECE : PIECE + DIAG, :].astype(F32), 0.0)
        for n, (i, j) in ((6, (0, 1)), (7, (2, 3))):
            t = piece_tile(n)
            tt = t.T
            d0, d1 = dg[i : i + 1, :], dg[j : j + 1, :]
            roots_new[slot, tile_of(i), tile_of(i)] = jnp.where(
                above, t, jnp.where(below, tt, d0)
            ).astype(BF16)
            roots_new[slot, tile_of(j), tile_of(j)] = jnp.where(
                below, t, jnp.where(above, tt, d1)
            ).astype(BF16)

    for k in range(1, n_mp):
        s2_cp(k).wait_recv()
    for k in range(1, n_mp):
        mine = mine + s2_in[k]
    ratio = jnp.sqrt(mine[:, :1]) / jnp.sqrt(mine[:, T - 1 :] + 1e-06)
    for b in range(4):
        update[b] = precond[b] * ratio

    @pl.when(even)
    def _():
        for cp in y_cp:
            cp.wait_send()
        ycopy().wait_send()
        for k in (1, 3, 2):
            ring_cp(0, k).wait_send()
        ring_cp(1, 2).wait_send()

    @pl.when(jnp.logical_not(even))
    def _():
        for s in range(2):
            over_cp(s).wait_send()

    for row in range(2):
        for s in range(2):
            sib_cp(row, s).wait_send()
    for k in range(1, N_DP):
        s1_cp(k).wait_send()
    for k in range(1, n_mp):
        s2_cp(k).wait_send()


def store(u, a, b, r, u_out, a_out, b_out, r_out, sems):
    copies = [
        pltpu.make_async_copy(r, r_out.at[0, 0], sems.at[0]),
        pltpu.make_async_copy(u, u_out, sems.at[1]),
        pltpu.make_async_copy(a, a_out, sems.at[2]),
        pltpu.make_async_copy(b, b_out, sems.at[3]),
    ]
    for cp in copies:
        cp.start()
    for cp in copies:
        cp.wait()


def per_device(grads, owners, roots_prev, moment_first, moment_second):
    n_mp = lax.axis_size("mp")
    hbm = pl.BlockSpec(memory_space=pltpu.HBM)
    any_spec = pl.BlockSpec(memory_space=pl.ANY)
    vmem = pl.BlockSpec(memory_space=pltpu.VMEM)
    small = jax.ShapeDtypeStruct((4, ROWS, BS), F32)

    def body(*refs):
        kernel(n_mp, *refs)

    update, m1n, m2n, roots_new = pl.pallas_call(
        body,
        out_shape=(small, small, small, jax.ShapeDtypeStruct((2, BS, BS), BF16)),
        in_specs=[pl.BlockSpec(memory_space=pltpu.SMEM), hbm, hbm, hbm, hbm],
        out_specs=(vmem, vmem, vmem, vmem),
        scratch_shapes=[
            pltpu.VMEM((4, BS, BS), BF16),
            pltpu.VMEM((2, BS, BS), BF16),
            pltpu.VMEM((BS, BS), BF16),
            pltpu.VMEM((4, BS, BS), BF16),
            pltpu.VMEM((2, BS, BS), BF16),
            pltpu.VMEM((2, 2, PIECE, T), BF16),
            pltpu.VMEM((2, 3, PIECE, T), BF16),
            pltpu.VMEM((PIECE, T), BF16),
            pltpu.VMEM((PIECE, T), BF16),
            pltpu.VMEM((2, 2, 8, T), F32),
            pltpu.VMEM((8, 8, T), F32),
            pltpu.VMEM((3, BS, T), F32),
            pltpu.VMEM((3, BS, T), F32),
            pltpu.VMEM((BS, T), F32),
            pltpu.VMEM((BS, T), BF16),
            pltpu.VMEM((4, ROWS, BS), F32),
            pltpu.VMEM((4, ROWS, BS), BF16),
            pltpu.VMEM((8, PIECE + DIAG, T), BF16),
            pltpu.VMEM((BS, BS), F32),
            pltpu.VMEM((BS, BS), BF16),
            pltpu.VMEM((BS, BS), F32),
            pltpu.VMEM((BS, BS), BF16),
            pltpu.VMEM((BS, BS), F32),
            pltpu.VMEM((BS, BS), BF16),
            pltpu.VMEM((4, ROWS, BS), F32),
            pltpu.VMEM((1, T), F32),
            pltpu.VMEM((N_DP, 1, T), F32),
            pltpu.VMEM((1, T), F32),
            pltpu.VMEM((max(n_mp, 2), 1, T), F32),
            pltpu.VMEM((4, ROWS, BS), F32),
            pltpu.VMEM((4, ROWS, BS), F32),
            pltpu.SemaphoreType.DMA((N_SEM,)),
            pltpu.SemaphoreType.DMA((N_SEM,)),
            pltpu.SemaphoreType.DMA((LOC,)),
        ],
        compiler_params=pltpu.CompilerParams(
            collective_id=0, has_side_effects=True, vmem_limit_bytes=62 * 2**20
        ),
        name="shampoo",
    )(owners.T, grads, roots_prev, moment_first, moment_second)
    return pl.pallas_call(
        store,
        out_shape=(small, small, small, jax.ShapeDtypeStruct((1, 1, 2, BS, BS), BF16)),
        in_specs=[vmem] * 4,
        out_specs=[hbm] * 4,
        scratch_shapes=[pltpu.SemaphoreType.DMA((4,))],
        name="store",
    )(update, m1n, m2n, roots_new)


def solution(mesh):
    return jax.shard_map(
        per_device,
        mesh=mesh,
        in_specs=(
            P("dp", "mp", None, None),
            P("mp", None),
            P("mp", None, None, None),
            P("mp", "dp", None),
            P("mp", "dp", None),
        ),
        out_specs=(
            P("mp", "dp", None),
            P("mp", "dp", None),
            P("mp", "dp", None),
            P("dp", "mp", None, None, None),
        ),
        check_vma=False,
    )
```
